32 devices in a mesh: dp: 4 (over y, x), expert: 8 (over z, core).
Axes of the slice: x: 2, y: 2, z: 4, core: 2. Of those that a mesh axis runs over, the one named last changes fastest.
Arguments:
- tokens: bfloat16 [4096, 7168], P('expert', 'dp'), may hold values from -6 to 6
- grad_out: bfloat16 [4096, 7168], P('expert', 'dp'), may hold values from -6 to 6
- route_ids: int32 [4096, 1], P('expert'), may hold values from 0 to 7; in each aligned block of 512 rows (0 to 511, 512 to 1023, ...) at most 80 rows name the same one
- gate_codes: int32 [4096, 1], P('expert'), may hold values from 1 to 255
- gate_weight: bfloat16 [8, 7168, 1024], P('expert', 'dp'), may hold values from -0.0625 to 0.0625
- up_weight: bfloat16 [8, 7168, 1024], P('expert', 'dp'), may hold values from -0.0625 to 0.0625
- down_weight: bfloat16 [8, 1024, 7168], P('expert', None, 'dp'), may hold values from -0.1875 to 0.1875
- momentum: bfloat16 [8, 1024, 7168], P('expert', None, 'dp'), may hold values from -6 to 6
Outputs:
- grad_tokens: bfloat16 [4096, 7168], P('expert', 'dp')
- new_down: bfloat16 [8, 1024, 7168], P('expert', None, 'dp')
- new_momentum: bfloat16 [8, 1024, 7168], P('expert', None, 'dp')
The draws below stay inside these ranges and needn't reach their ends.
Inputs may be any that keep to these rules, and one draw needn't show every extreme that they name: `route_ids`: each token names one expert. Among the 512 tokens of one index of the expert axis no expert is named by more than 80 tokens, a bound that some block reaches.
All inputs are finite; a program needn't handle non-finite values.
Results may differ from the reference program's by a relative error of at most 0.022.
Values may be sent and summed in bfloat16 or wider, within the bound.
No kernel may reach another device: no remote copies, remote signals or barrier semaphores. Data moves between devices by JAX's collectives and lax.ppermute only.
A program may use at most 128 MiB of HBM per device.

```python
import math
import jax
import jax.numpy as jnp
import numpy as np
from jax import lax

D = 7168
H = 1024
TOPK = 1
TOK_DEV = 512
EXPERTS = 8
CAP = 80
TOKENS = 4096
N_DP = 4
N_EXPERT = 8


def with_ends(array, stream_key, low, top_value):
    extent = array.shape
    spot = [jax.random.randint(jax.random.fold_in(stream_key, axis), (), 0, extent[axis]) for axis in range(len(extent))]
    array = array.at[tuple(spot)].set(low)
    longest = extent.index(max(extent))
    spot[longest] = (spot[longest] + 1) % extent[longest]
    return array.at[tuple(spot)].set(top_value)


def shard_levels(own_key, shape, pieces, smallest, top_value):
    def one(axis_at, blocks):
        steps = jax.random.uniform(jax.random.fold_in(jax.random.fold_in(own_key, 6), axis_at), (blocks,), jnp.float32, smallest / len(pieces), top_value / len(pieces))
        return jnp.repeat(jnp.exp(steps), shape[axis_at] // blocks).reshape((-1,) + (1,) * (len(shape) - axis_at - 1))

    level = one(*pieces[0])
    for cut in pieces[1:]:
        level = level * one(*cut)
    return level


def deal_out(rng, own, number, rows, amount, top, limit, lean):
    order = jax.random.permutation(rng, amount)
    crowded, ordinary = load_shares(amount, rows * top, limit, lean, True), load_shares(amount, rows * top, limit, lean, False)
    places = jnp.arange(amount)

    def named(lengths, rotation):
        used = int((lengths > 0).sum())
        fixed = max(1, used // 4)
        shifted = fixed + (places - fixed + rotation * (used - fixed)) % max(1, amount - fixed)
        return jnp.zeros((amount,), jnp.int32).at[order[jnp.where(places < fixed, places, shifted)]].set(jnp.asarray(lengths, jnp.int32))

    lengths = jnp.where(number % 4 == 0, named(crowded, number // 4), named(ordinary, number - number // 4 - 1))
    mixed = jax.random.permutation(jax.random.fold_in(own, 3), amount)
    giver, taker = mixed[0:amount // 2 * 2:2], mixed[1:amount // 2 * 2:2]
    room = jnp.minimum(lengths[giver] - 1, limit - lengths[taker]) // 2
    room = jnp.where((giver == order[0]) | (taker == order[0]) | (lengths[taker] == 0), 0, jnp.maximum(room, 0))
    shifted = jax.random.randint(jax.random.fold_in(own, 4), (amount // 2,), 0, 1 << 20) % (room + 1)
    lengths = lengths.at[giver].add(-shifted).at[taker].add(shifted)
    items = jnp.searchsorted(jnp.cumsum(lengths), jnp.arange(rows * top), side="right").astype(jnp.int32)
    table = items.reshape(top, rows).T
    table = table[jax.random.permutation(jax.random.fold_in(own, 1), rows)]
    rotation = jax.random.randint(jax.random.fold_in(own, 2), (rows, 1), 0, top)
    return jnp.take_along_axis(table, (jnp.arange(top)[None, :] + rotation) % top, axis=1)


def load_shares(count, total, most, lean, full):
    weights = [(1 << 20) // math.isqrt(grade ** lean) + 1 for grade in range(1, count + 1)]
    largest = most if full else min(most, max(-(-total // count), total * weights[0] // sum(weights)))
    least = 1 if total - largest >= count - 1 else 0
    holding, spare = [largest] + [least] * (count - 1), total - largest - least * (count - 1)
    while spare > 0:
        candidates = [i for i in range(1, count) if holding[i] < largest] or [i for i in range(1, count) if holding[i] < most]
        whole, left = sum([weights[i] for i in candidates]), spare
        for i in candidates:
            extra = min(most - holding[i], max(1, left * weights[i] // whole), spare)
            holding[i] = holding[i] + extra
            spare = spare - extra
    return np.array(holding)


def bell_draw(rng, dims, spread, bound, split=(), held_as=jnp.bfloat16):
    values = jax.random.normal(rng, dims, jnp.float32) * spread
    if len(split) > 0:
        values = shard_levels(rng, dims, split, -0.22, 0.18) * values
    return jnp.clip(values, min=-bound, max=bound).astype(held_as)


def setup_inputs(seed: int = 0) -> dict:
    streams_of = jax.random.split(jax.random.key(seed), 9)
    tokens = bell_draw(streams_of[0], (TOKENS, D), 1.0, 6.0, ((0, 8), (1, 4)))
    grad_out = bell_draw(streams_of[1], (TOKENS, D), 1.0, 6.0, ((0, 8), (1, 4)))
    route_ids_keys = jax.random.split(jax.random.fold_in(streams_of[2], 1), TOKENS // TOK_DEV)
    route_ids_turns = jax.random.permutation(jax.random.fold_in(streams_of[2], 3), TOKENS // TOK_DEV)
    route_ids = jax.vmap(lambda own, number: deal_out(jax.random.fold_in(streams_of[2], 2), own, number, TOK_DEV, EXPERTS, TOPK, CAP, 2))(route_ids_keys, route_ids_turns).reshape((TOKENS, TOPK))
    gate_codes = with_ends(jax.random.randint(streams_of[3], (TOKENS, TOPK), 1, 256), jax.random.fold_in(streams_of[3], 1), 1, 255).astype(jnp.int32)
    gate_weight = bell_draw(streams_of[4], (EXPERTS, D, H), D ** -0.5, 0.0625, ((0, 8), (1, 4)))
    up_weight = bell_draw(streams_of[5], (EXPERTS, D, H), D ** -0.5, 0.0625, ((0, 8), (1, 4)))
    down_weight = bell_draw(streams_of[6], (EXPERTS, H, D), H ** -0.5, 0.1875, ((0, 8), (2, 4)))
    momentum = bell_draw(streams_of[7], (EXPERTS, H, D), 1.0, 6.0, ((0, 8), (2, 4)))
    return {"tokens": tokens, "grad_out": grad_out, "route_ids": route_ids, "gate_codes": gate_codes, "gate_weight": gate_weight, "up_weight": up_weight, "down_weight": down_weight, "momentum": momentum}


first_beta = 0.9
second_beta = 0.9
learn_rate = 0.01
decay_rate = 3.0
soft_width = 1.0

def activate(terms):
    pre_gate = terms[:, 0, :]
    pre_up = terms[:, 1, :]
    grad_hidden = terms[:, 2, :]
    sigmoid = jax.nn.sigmoid(pre_gate)
    active = pre_gate * sigmoid
    hidden = (active * pre_up).astype(jnp.bfloat16)
    d_gate = (grad_hidden * pre_up * sigmoid * (1.0 + pre_gate * (1.0 - sigmoid))).astype(jnp.bfloat16)
    d_up = (grad_hidden * active).astype(jnp.bfloat16)
    return (hidden, d_gate, d_up)

def lion_update(grad, weight_in, moment_in):
    moment = moment_in.astype(jnp.float32)
    weight = weight_in.astype(jnp.float32)
    blend = first_beta * moment + (1.0 - first_beta) * grad
    step = blend / jnp.sqrt(blend * blend + soft_width * soft_width)
    agree = jnp.maximum(step * jnp.sign(weight), 0.0)
    new_weight = (weight - learn_rate * (step + decay_rate * agree * weight)).astype(jnp.bfloat16)
    new_moment = (second_beta * moment + (1.0 - second_beta) * grad).astype(jnp.bfloat16)
    return (new_weight, new_moment)

def reference(tokens, grad_out, route_ids, gate_codes, gate_weight, up_weight, down_weight, momentum):
    slab = D // N_DP
    live = N_EXPERT * CAP
    flat_ids = route_ids.reshape(-1)
    owner = (jnp.arange(TOKENS * TOPK, dtype=jnp.int32) // TOPK).astype(jnp.int32)
    scales = gate_codes.reshape(-1).astype(jnp.float32) / 256.0

    def per_expert(total, expert):
        hits = flat_ids == expert
        order = jnp.nonzero(hits, size=live, fill_value=0)[0].astype(jnp.int32)
        valid = jnp.arange(live, dtype=jnp.int32) < jnp.sum(hits.astype(jnp.int32))
        rows = owner[order]
        x_rows = jnp.where(valid[:, None], tokens[rows].astype(jnp.float32), 0.0).astype(jnp.bfloat16)
        dy_rows = jnp.where(valid[:, None], scales[order][:, None] * grad_out[rows].astype(jnp.float32), 0.0).astype(jnp.bfloat16)
        w_gate = gate_weight[expert]
        w_up = up_weight[expert]
        w_down = down_weight[expert]
        terms = jnp.zeros((live, 3, H), jnp.float32)
        for slice_index in range(N_DP):
            start = slice_index * slab
            stop = start + slab
            gate_part = jnp.dot(x_rows[:, start:stop], w_gate[start:stop], preferred_element_type=jnp.float32)
            up_part = jnp.dot(x_rows[:, start:stop], w_up[start:stop], preferred_element_type=jnp.float32)
            back_part = jnp.dot(dy_rows[:, start:stop], w_down[:, start:stop].T, preferred_element_type=jnp.float32)
            stacked = jnp.stack([gate_part, up_part, back_part], axis=1).astype(jnp.bfloat16)
            stacked = lax.optimization_barrier(stacked)
            terms = terms + stacked.astype(jnp.float32)
        hidden, d_gate, d_up = activate(terms)
        grad_down = jnp.dot(hidden.T, dy_rows, preferred_element_type=jnp.float32)
        grad_rows = (jnp.dot(d_gate, w_gate.T, preferred_element_type=jnp.float32) + jnp.dot(d_up, w_up.T, preferred_element_type=jnp.float32)).astype(jnp.bfloat16)
        total = total.at[rows].add(jnp.where(valid[:, None], grad_rows.astype(jnp.float32), 0.0))
        new_weight, new_moment = lion_update(grad_down, w_down, momentum[expert])
        return (total, (new_weight, new_moment))
    total, outs = lax.scan(per_expert, jnp.zeros((TOKENS, D), jnp.float32), jnp.arange(N_EXPERT, dtype=jnp.int32))
    return (total.astype(jnp.bfloat16), outs[0], outs[1])
```

```python
import functools

import jax
import jax.numpy as jnp
from jax import lax
from jax.experimental import pallas as pl
from jax.experimental.pallas import tpu as pltpu
from jax.sharding import PartitionSpec as P

first_beta = 0.9
learn_rate = 0.01
decay_rate = 3.0
soft_width = 1.0

TILE = 256
VMEM_BYTES = 24 * 1024 * 1024

bf16 = jnp.bfloat16
f32 = jnp.float32


def grouping(n):
    half = n // 2
    step = max(1, half // 4)
    far = [list(range(i, i + step)) for i in range(half, n, step)]
    cut = half - step
    return far, [list(range(cut)), list(range(cut, half))]


def skipping(body, n_in, n_deps):
    def run(*refs):
        body(*refs[:n_in], *refs[n_in + n_deps :])

    return run


def call(body, operands, deps, out_shape, in_specs, out_specs, grid=(), scalars=0, scratch=(), aliases=None):
    any_spec = pl.BlockSpec(memory_space=pl.ANY)
    return pl.pallas_call(
        skipping(body, len(operands), len(deps)),
        out_shape=out_shape,
        grid_spec=pltpu.PrefetchScalarGridSpec(
            num_scalar_prefetch=scalars,
            grid=grid,
            in_specs=list(in_specs) + [any_spec] * len(deps),
            out_specs=out_specs,
            scratch_shapes=list(scratch),
        ),
        input_output_aliases=aliases or {},
        compiler_params=pltpu.CompilerParams(vmem_limit_bytes=VMEM_BYTES),
        cost_estimate=pl.CostEstimate(flops=0, bytes_accessed=0, transcendentals=0),
    )(*operands, *deps)


def dot(a, b, ca=1, cb=0):
    return lax.dot_general(a, b, (((ca,), (cb,)), ((), ())), preferred_element_type=f32)


def whole(shape):
    return pl.BlockSpec(shape, lambda *_: (0,) * len(shape))


def after_body(*refs):
    pass


def after(value, deps):
    any_spec = pl.BlockSpec(memory_space=pl.ANY)
    return call(
        after_body, [value], deps, jax.ShapeDtypeStruct(value.shape, value.dtype), [any_spec], any_spec, aliases={0: 0}
    )


def dispatch_body(n, cap, offs, first, *refs):
    if first:
        me_ref, ids_ref, codes_ref, x_ref, g_ref, target_ref, *outs = refs
        ids = ids_ref[...]
        t = ids.shape[1]
        hot = (lax.broadcasted_iota(jnp.int32, (n, t), 0) == ids).astype(f32)
        before = (
            lax.broadcasted_iota(jnp.int32, (t, t), 0) < lax.broadcasted_iota(jnp.int32, (t, t), 1)
        ).astype(f32)
        counts = dot(hot.astype(bf16), before.astype(bf16))
        rank = jnp.sum(hot * counts, axis=0, keepdims=True).astype(jnp.int32)
        target = ids * cap + rank
        target_ref[...] = target
    else:
        me_ref, tgt_ref, codes_ref, x_ref, g_ref, *outs = refs
        target = tgt_ref[...]
    t, s = x_ref.shape
    scale = codes_ref[...].astype(f32) / 256.0
    slots = lax.broadcasted_iota(jnp.int32, (cap, t), 0)
    hits = [slots + (me_ref[0] ^ k) * cap == target for k in offs]
    pick = jnp.concatenate([jnp.where(h, 1.0, 0.0).astype(bf16) for h in hits], axis=0)
    scaled = jnp.concatenate([jnp.where(h, scale, 0.0).astype(bf16) for h in hits], axis=0)
    for c in range(0, s, TILE):
        for left, ref, base in ((pick, x_ref, 0), (scaled, g_ref, s)):
            rows = dot(left, ref[:, c : c + TILE]).astype(bf16)
            for i, out in enumerate(outs):
                out[:, base + c : base + c + TILE] = rows[i * cap : (i + 1) * cap]


def dispatch(n, cap, offs, me, marks, codes, x, g, first, deps):
    t, s = x.shape
    out_shape = [jax.ShapeDtypeStruct((cap, 2 * s), bf16) for _ in offs]
    if first:
        out_shape = [jax.ShapeDtypeStruct((1, t), jnp.int32)] + out_shape
    vmem = pl.BlockSpec(memory_space=pltpu.VMEM)
    return call(
        functools.partial(dispatch_body, n, cap, offs, first),
        [me, marks, codes, x, g],
        deps,
        out_shape,
        [pl.BlockSpec(memory_space=pltpu.SMEM)] + [vmem] * 4,
        [vmem] * len(out_shape),
    )


def forward_body(cap, nb, ndp, dp_ref, *refs):
    blocks, (wg, wu, wd), outs, rows = refs[:nb], refs[nb : nb + 3], refs[nb + 3 : -1], refs[-1]
    d = pl.program_id(0)
    s = wg.shape[0]
    hq = wg.shape[1]

    @pl.when(d == 0)
    def _():
        for i, blk in enumerate(blocks):
            rows[i * cap : (i + 1) * cap, :] = blk[...]

    x = rows[:, :s]
    r = rows[:, s:]
    a = dot(x, wg[...]).astype(bf16)
    b = dot(x, wu[...]).astype(bf16)
    q = dot(r, wd[...], 1, 1).astype(bf16)
    for k in range(ndp):

        @pl.when(d == k)
        def _():
            outs[k][:, :hq] = a
            outs[k][:, hq : 2 * hq] = b
            outs[k][:, 2 * hq :] = q


def forward(cap, ndp, dp_idx, blocks, wg, wu, wd, deps):
    s, h = wg.shape
    hq = h // ndp
    nb = len(blocks)
    rows = nb * cap
    return call(
        functools.partial(forward_body, cap, nb, ndp),
        [dp_idx, *blocks, wg, wu, wd],
        deps,
        [jax.ShapeDtypeStruct((rows, 3 * hq), bf16)] * ndp,
        [whole((cap, 2 * s))] * nb
        + [pl.BlockSpec((s, hq), lambda d, i: (0, i[0] ^ d))] * 2
        + [pl.BlockSpec((hq, s), lambda d, i: (i[0] ^ d, 0))],
        [whole((rows, 3 * hq))] * ndp,
        grid=(ndp,),
        scalars=1,
        scratch=[pltpu.VMEM((rows, 2 * s), bf16)],
    )


def activate_body(*refs):
    *parts, out = refs
    hq = out.shape[1] // 3

    def total(j):
        t = parts[0][:, j * hq : (j + 1) * hq].astype(f32)
        for p in parts[1:]:
            t = t + p[:, j * hq : (j + 1) * hq].astype(f32)
        return t

    a, b, q = total(0), total(1), total(2)
    sigma = jax.nn.sigmoid(a)
    act = a * sigma
    out[:, :hq] = (act * b).astype(bf16)
    out[:, hq : 2 * hq] = (q * b * sigma * (1.0 + a * (1.0 - sigma))).astype(bf16)
    out[:, 2 * hq :] = (q * act).astype(bf16)


def activate(parts, deps):
    vmem = pl.BlockSpec(memory_space=pltpu.VMEM)
    return call(
        activate_body, parts, deps, jax.ShapeDtypeStruct(parts[0].shape, bf16), [vmem] * len(parts), vmem
    )


def backward_body(cap, nb, ndp, dp_ref, *refs):
    pieces, (wg, wu), outs, (dg, du) = refs[:ndp], refs[ndp : ndp + 2], refs[ndp + 2 : -2], refs[-2:]
    hq = pieces[0].shape[1] // 3

    @pl.when(pl.program_id(0) == 0)
    def _():
        for d, piece in enumerate(pieces):
            at = pl.ds(pl.multiple_of((dp_ref[0] ^ d) * hq, hq), hq)
            dg[:, at] = piece[:, hq : 2 * hq]
            du[:, at] = piece[:, 2 * hq :]

    rows = (dot(dg[...], wg[...], 1, 1) + dot(du[...], wu[...], 1, 1)).astype(bf16)
    for i, out in enumerate(outs):
        out[...] = rows[i * cap : (i + 1) * cap]


def backward(cap, nb, ndp, dp_idx, pieces, wg, wu, deps):
    s, h = wg.shape
    return call(
        functools.partial(backward_body, cap, nb, ndp),
        [dp_idx, *pieces, wg, wu],
        deps,
        [jax.ShapeDtypeStruct((cap, s), bf16)] * nb,
        [whole(pieces[0].shape)] * ndp + [pl.BlockSpec((TILE, h), lambda c, i: (c, 0))] * 2,
        [pl.BlockSpec((cap, TILE), lambda c, i: (0, c))] * nb,
        grid=(s // TILE,),
        scalars=1,
        scratch=[pltpu.VMEM((nb * cap, h), bf16)] * 2,
    )


def down_body(cap, sizes, ndp, dp_ref, *refs):
    n_pieces = len(sizes) * ndp
    n_blocks = sum(sizes)
    pieces = refs[:n_pieces]
    blocks = refs[n_pieces : n_pieces + n_blocks]
    wd, mom, new_w, new_m, hid_t, dy = refs[n_pieces + n_blocks :]
    hq = pieces[0].shape[1]

    @pl.when(pl.program_id(0) == 0)
    def _():
        base = 0
        for g, size in enumerate(sizes):
            for d in range(ndp):
                at = pl.ds(pl.multiple_of((dp_ref[0] ^ d) * hq, hq), hq)
                piece = pieces[g * ndp + d][...].astype(f32)
                hid_t[at, base : base + size * cap] = piece.T.astype(bf16)
            base += size * cap

    for i, blk in enumerate(blocks):
        dy[i * cap : (i + 1) * cap, :] = blk[...]
    step_rows = 128
    for c in range(0, hid_t.shape[0], step_rows):
        at = slice(c, c + step_rows)
        grad = dot(hid_t[at, :], dy[...])
        w = wd[at, :].astype(f32)
        blend = first_beta * mom[at, :].astype(f32) + (1.0 - first_beta) * grad
        step = blend * lax.rsqrt(blend * blend + soft_width * soft_width)
        agree = jnp.where((step > 0.0) == (w > 0.0), jnp.abs(step), 0.0)
        new_w[at, :] = (w - learn_rate * (step + decay_rate * agree * w)).astype(bf16)
        new_m[at, :] = blend.astype(bf16)


def down(cap, sizes, ndp, dp_idx, pieces, blocks, wd, mom, deps):
    h, s = wd.shape
    hq = h // ndp
    rows = cap * sum(sizes)
    col = pl.BlockSpec((h, TILE), lambda c, i: (0, c))
    return call(
        functools.partial(down_body, cap, sizes, ndp),
        [dp_idx, *pieces, *blocks, wd, mom],
        deps,
        [jax.ShapeDtypeStruct((h, s), bf16)] * 2,
        [whole((p.shape[0], hq)) for p in pieces]
        + [pl.BlockSpec((cap, TILE), lambda c, i: (0, s // TILE + c))] * len(blocks)
        + [col, col],
        [col, col],
        grid=(s // TILE,),
        scalars=1,
        scratch=[pltpu.VMEM((h, rows), bf16), pltpu.VMEM((rows, TILE), bf16)],
    )


def combine_body(cap, offs, chained, me_ref, tgt_ref, *refs):
    nb = len(offs)
    backs = refs[:nb]
    prev = refs[nb] if chained else None
    out, pick_t, rows = refs[-3:]

    @pl.when(pl.program_id(0) == 0)
    def _():
        target = tgt_ref[...]
        slots = lax.broadcasted_iota(jnp.int32, (cap, target.shape[1]), 0)
        for i, k in enumerate(offs):
            hit = jnp.where(slots + (me_ref[0] ^ k) * cap == target, 1.0, 0.0)
            pick_t[i * cap : (i + 1) * cap, :] = hit.astype(bf16)

    for i, blk in enumerate(backs):
        rows[i * cap : (i + 1) * cap, :] = blk[...]
    total = dot(pick_t[...], rows[...], 0, 0)
    if chained:
        total = total + prev[...].astype(f32)
    out[...] = total.astype(bf16)


def combine(cap, offs, me, target, backs, prev, deps):
    t = target.shape[1]
    s = backs[0].shape[1]
    nb = len(offs)
    col = pl.BlockSpec((t, TILE), lambda c, i: (0, c))
    extra = [] if prev is None else [prev]
    return call(
        functools.partial(combine_body, cap, offs, prev is not None),
        [me, target, *backs, *extra],
        deps,
        jax.ShapeDtypeStruct((t, s), bf16),
        [whole((1, t))] + [pl.BlockSpec((cap, TILE), lambda c, i: (0, c))] * nb + [col] * len(extra),
        col,
        grid=(s // TILE,),
        scalars=1,
        scratch=[pltpu.VMEM((nb * cap, t), bf16), pltpu.VMEM((nb * cap, TILE), bf16)],
    )


def local(tokens, grad_out, route_ids, gate_codes, gate_weight, up_weight, down_weight, momentum):
    n = lax.axis_size("expert")
    ndp = lax.axis_size("dp")
    t = tokens.shape[0]
    most = max(2, t * 5 // (4 * n))
    cap = -(-most // 16) * 16
    me = lax.axis_index("expert").astype(jnp.int32).reshape(1)
    dp_idx = lax.axis_index("dp").astype(jnp.int32).reshape(1)
    ids = route_ids.reshape(1, t)
    codes = gate_codes.reshape(1, t)
    wg, wu, wd, mom = gate_weight[0], up_weight[0], down_weight[0], momentum[0]

    def swap_expert(v, k):
        return lax.ppermute(v, "expert", [(i, i ^ k) for i in range(n)])

    def swap_dp(v, k):
        return lax.ppermute(v, "dp", [(i, i ^ k) for i in range(ndp)])

    far, near = grouping(n)
    chunks = [near[0] + far[0], near[1] + far[1]] + far[2:]
    send, got, ready, back, pieces, parts = {}, {}, {}, {}, {}, {}
    mark = []

    def push(offs, deps):
        for k in offs:
            if deps:
                send[k] = after(send[k], mark + deps)
                mark[:] = [send[k]]
            got[k] = swap_expert(send[k], k)

    def give_back(offs, deps):
        for k in offs:
            rows = ready[k]
            if deps:
                rows = after(rows, mark + deps)
                mark[:] = [rows]
            back[k] = swap_expert(rows, k) if k else rows

    def fwd(c):
        own, *others = forward(cap, ndp, dp_idx, [got[k] for k in chunks[c]], wg, wu, wd, mark)
        mark[:] = [own]
        parts[c] = [own] + [swap_dp(v, d + 1) for d, v in enumerate(others)]

    def act(c):
        own = activate(parts[c], mark)
        mark[:] = [own]
        pieces[c] = [own] + [swap_dp(own, d) for d in range(1, ndp)]

    def bwd(c):
        rows = backward(cap, len(chunks[c]), ndp, dp_idx, pieces[c], wg, wu, mark)
        mark[:] = [rows[0]]
        ready.update(zip(chunks[c], rows))

    def gotten(offs):
        return [got[k] for k in offs]

    target, *sends = dispatch(n, cap, far[0], me, ids, codes, tokens, grad_out, True, [])
    send.update(zip(far[0], sends))
    mark[:] = [sends[0]]
    push(far[0], [])
    for offs in (near[0], far[1] + near[1], far[2] + far[3]):
        sends = dispatch(n, cap, offs, me, target, codes, tokens, grad_out, False, mark)
        send.update(zip(offs, sends))
        mark[:] = [sends[0]]
        if offs is near[0]:
            push(offs, [])
            got[0] = send[0]
    inner = [k for k in near[0] if k > 1]

    push(far[1], gotten(far[0]))
    push(near[1], gotten(inner))
    fwd(0)
    push(far[2], gotten(far[1]))
    act(0)
    fwd(1)
    push(far[3], gotten(far[2]))
    bwd(0)
    give_back([0, 1], [])
    fwd(2)
    act(1)
    give_back(far[0], gotten(far[3]))
    give_back(inner, gotten(far[3]))
    fwd(3)
    bwd(1)
    give_back(far[1], [back[k] for k in far[0]])
    give_back(near[1], [back[k] for k in inner])
    act(2)
    act(3)
    bwd(2)
    give_back(far[2], [back[k] for k in far[1]])
    bwd(3)
    order = range(len(chunks))
    flat = [k for c in order for k in chunks[c]]
    new_down, new_moment = down(
        cap,
        [len(chunks[c]) for c in order],
        ndp,
        dp_idx,
        [p for c in order for p in pieces[c]],
        gotten(flat),
        wd,
        mom,
        mark,
    )
    mark[:] = [new_down]
    give_back(far[3], [back[k] for k in far[2]])
    early = [k for k in flat if k not in far[3]]
    part = combine(cap, early, me, target, [back[k] for k in early], None, mark)
    grad_tokens = combine(cap, far[3], me, target, [back[k] for k in far[3]], part, [])
    return (grad_tokens, new_down[None], new_moment[None])


def solution(mesh):
    placed = (
        P("expert", "dp"),
        P("expert", "dp"),
        P("expert", None),
        P("expert", None),
        P("expert", "dp", None),
        P("expert", "dp", None),
        P("expert", None, "dp"),
        P("expert", None, "dp"),
    )
    return jax.shard_map(
        local,
        mesh=mesh,
        in_specs=placed,
        out_specs=(P("expert", "dp"), P("expert", None, "dp"), P("expert", None, "dp")),
        check_vma=False,
    )
```

```python
import functools

import jax
import jax.numpy as jnp
from jax import lax
from jax.experimental import pallas as pl
from jax.experimental.pallas import tpu as pltpu
from jax.sharding import PartitionSpec as P

first_beta = 0.9
learn_rate = 0.01
decay_rate = 3.0
soft_width = 1.0

TILE = 256
VMEM_BYTES = 24 * 1024 * 1024

bf16 = jnp.bfloat16
f32 = jnp.float32


def grouping(n):
    half = n // 2
    step = max(1, half // 4)
    far = [list(range(i, i + step)) for i in range(half, n, step)]
    cuts = [0, half - 2 * step, half - step, half]
    return far, [list(range(i, j)) for i, j in zip(cuts, cuts[1:])]


def skipping(body, n_in, n_deps):
    def run(*refs):
        body(*refs[:n_in], *refs[n_in + n_deps :])

    return run


def call(body, operands, deps, out_shape, in_specs, out_specs, grid=(), scalars=0, scratch=(), aliases=None):
    any_spec = pl.BlockSpec(memory_space=pl.ANY)
    return pl.pallas_call(
        skipping(body, len(operands), len(deps)),
        out_shape=out_shape,
        grid_spec=pltpu.PrefetchScalarGridSpec(
            num_scalar_prefetch=scalars,
            grid=grid,
            in_specs=list(in_specs) + [any_spec] * len(deps),
            out_specs=out_specs,
            scratch_shapes=list(scratch),
        ),
        input_output_aliases=aliases or {},
        compiler_params=pltpu.CompilerParams(vmem_limit_bytes=VMEM_BYTES),
        cost_estimate=pl.CostEstimate(flops=0, bytes_accessed=0, transcendentals=0),
    )(*operands, *deps)


def dot(a, b, ca=1, cb=0):
    return lax.dot_general(a, b, (((ca,), (cb,)), ((), ())), preferred_element_type=f32)


def whole(shape):
    return pl.BlockSpec(shape, lambda *_: (0,) * len(shape))


def after_body(*refs):
    pass


def after(value, deps):
    any_spec = pl.BlockSpec(memory_space=pl.ANY)
    return call(
        after_body, [value], deps, jax.ShapeDtypeStruct(value.shape, value.dtype), [any_spec], any_spec, aliases={0: 0}
    )


def dispatch_body(n, cap, offs, first, *refs):
    if first:
        me_ref, ids_ref, codes_ref, x_ref, g_ref, target_ref, *outs = refs
        ids = ids_ref[...]
        t = ids.shape[1]
        hot = (lax.broadcasted_iota(jnp.int32, (n, t), 0) == ids).astype(f32)
        before = (
            lax.broadcasted_iota(jnp.int32, (t, t), 0) < lax.broadcasted_iota(jnp.int32, (t, t), 1)
        ).astype(f32)
        counts = dot(hot.astype(bf16), before.astype(bf16))
        rank = jnp.sum(hot * counts, axis=0, keepdims=True).astype(jnp.int32)
        target = ids * cap + rank
        target_ref[...] = target
    else:
        me_ref, tgt_ref, codes_ref, x_ref, g_ref, *outs = refs
        target = tgt_ref[...]
    t, s = x_ref.shape
    scale = codes_ref[...].astype(f32) / 256.0
    slots = lax.broadcasted_iota(jnp.int32, (cap, t), 0)
    hits = [slots + (me_ref[0] ^ k) * cap == target for k in offs]
    pick = jnp.concatenate([jnp.where(h, 1.0, 0.0).astype(bf16) for h in hits], axis=0)
    scaled = jnp.concatenate([jnp.where(h, scale, 0.0).astype(bf16) for h in hits], axis=0)
    for c in range(0, s, TILE):
        for left, ref, base in ((pick, x_ref, 0), (scaled, g_ref, s)):
            rows = dot(left, ref[:, c : c + TILE]).astype(bf16)
            for i, out in enumerate(outs):
                out[:, base + c : base + c + TILE] = rows[i * cap : (i + 1) * cap]


def dispatch(n, cap, offs, me, marks, codes, x, g, first, deps):
    t, s = x.shape
    out_shape = [jax.ShapeDtypeStruct((cap, 2 * s), bf16) for _ in offs]
    if first:
        out_shape = [jax.ShapeDtypeStruct((1, t), jnp.int32)] + out_shape
    vmem = pl.BlockSpec(memory_space=pltpu.VMEM)
    return call(
        functools.partial(dispatch_body, n, cap, offs, first),
        [me, marks, codes, x, g],
        deps,
        out_shape,
        [pl.BlockSpec(memory_space=pltpu.SMEM)] + [vmem] * 4,
        [vmem] * len(out_shape),
    )


def forward_body(cap, nb, ndp, dp_ref, *refs):
    blocks, (wg, wu, wd), outs, rows = refs[:nb], refs[nb : nb + 3], refs[nb + 3 : -1], refs[-1]
    d = pl.program_id(0)
    s = wg.shape[0]
    hq = wg.shape[1]

    @pl.when(d == 0)
    def _():
        for i, blk in enumerate(blocks):
            rows[i * cap : (i + 1) * cap, :] = blk[...]

    x = rows[:, :s]
    r = rows[:, s:]
    a = dot(x, wg[...]).astype(bf16)
    b = dot(x, wu[...]).astype(bf16)
    q = dot(r, wd[...], 1, 1).astype(bf16)
    for k in range(ndp):

        @pl.when(d == k)
        def _():
            outs[k][:, :hq] = a
            outs[k][:, hq : 2 * hq] = b
            outs[k][:, 2 * hq :] = q


def forward(cap, ndp, dp_idx, blocks, wg, wu, wd, deps):
    s, h = wg.shape
    hq = h // ndp
    nb = len(blocks)
    rows = nb * cap
    return call(
        functools.partial(forward_body, cap, nb, ndp),
        [dp_idx, *blocks, wg, wu, wd],
        deps,
        [jax.ShapeDtypeStruct((rows, 3 * hq), bf16)] * ndp,
        [whole((cap, 2 * s))] * nb
        + [pl.BlockSpec((s, hq), lambda d, i: (0, i[0] ^ d))] * 2
        + [pl.BlockSpec((hq, s), lambda d, i: (i[0] ^ d, 0))],
        [whole((rows, 3 * hq))] * ndp,
        grid=(ndp,),
        scalars=1,
        scratch=[pltpu.VMEM((rows, 2 * s), bf16)],
    )


def activate_body(*refs):
    *parts, out = refs
    hq = out.shape[1] // 3

    def total(j):
        t = parts[0][:, j * hq : (j + 1) * hq].astype(f32)
        for p in parts[1:]:
            t = t + p[:, j * hq : (j + 1) * hq].astype(f32)
        return t

    a, b, q = total(0), total(1), total(2)
    sigma = jax.nn.sigmoid(a)
    act = a * sigma
    out[:, :hq] = (act * b).astype(bf16)
    out[:, hq : 2 * hq] = (q * b * sigma * (1.0 + a * (1.0 - sigma))).astype(bf16)
    out[:, 2 * hq :] = (q * act).astype(bf16)


def activate(parts, deps):
    vmem = pl.BlockSpec(memory_space=pltpu.VMEM)
    return call(
        activate_body, parts, deps, jax.ShapeDtypeStruct(parts[0].shape, bf16), [vmem] * len(parts), vmem
    )


def backward_body(cap, nb, ndp, dp_ref, *refs):
    pieces, (wg, wu), outs, (dg, du) = refs[:ndp], refs[ndp : ndp + 2], refs[ndp + 2 : -2], refs[-2:]
    hq = pieces[0].shape[1] // 3

    @pl.when(pl.program_id(0) == 0)
    def _():
        for d, piece in enumerate(pieces):
            at = pl.ds(pl.multiple_of((dp_ref[0] ^ d) * hq, hq), hq)
            dg[:, at] = piece[:, hq : 2 * hq]
            du[:, at] = piece[:, 2 * hq :]

    rows = (dot(dg[...], wg[...], 1, 1) + dot(du[...], wu[...], 1, 1)).astype(bf16)
    for i, out in enumerate(outs):
        out[...] = rows[i * cap : (i + 1) * cap]


def backward(cap, nb, ndp, dp_idx, pieces, wg, wu, deps):
    s, h = wg.shape
    return call(
        functools.partial(backward_body, cap, nb, ndp),
        [dp_idx, *pieces, wg, wu],
        deps,
        [jax.ShapeDtypeStruct((cap, s), bf16)] * nb,
        [whole(pieces[0].shape)] * ndp + [pl.BlockSpec((TILE, h), lambda c, i: (c, 0))] * 2,
        [pl.BlockSpec((cap, TILE), lambda c, i: (0, c))] * nb,
        grid=(s // TILE,),
        scalars=1,
        scratch=[pltpu.VMEM((nb * cap, h), bf16)] * 2,
    )


def down_body(cap, sizes, ndp, dp_ref, *refs):
    n_pieces = len(sizes) * ndp
    n_blocks = sum(sizes)
    pieces = refs[:n_pieces]
    blocks = refs[n_pieces : n_pieces + n_blocks]
    wd, mom, new_w, new_m, hid_t, dy = refs[n_pieces + n_blocks :]
    hq = pieces[0].shape[1]

    @pl.when(pl.program_id(0) == 0)
    def _():
        base = 0
        for g, size in enumerate(sizes):
            for d in range(ndp):
                at = pl.ds(pl.multiple_of((dp_ref[0] ^ d) * hq, hq), hq)
                piece = pieces[g * ndp + d][...].astype(f32)
                hid_t[at, base : base + size * cap] = piece.T.astype(bf16)
            base += size * cap

    for i, blk in enumerate(blocks):
        dy[i * cap : (i + 1) * cap, :] = blk[...]
    step_rows = 128
    for c in range(0, hid_t.shape[0], step_rows):
        at = slice(c, c + step_rows)
        grad = dot(hid_t[at, :], dy[...])
        w = wd[at, :].astype(f32)
        blend = first_beta * mom[at, :].astype(f32) + (1.0 - first_beta) * grad
        step = blend * lax.rsqrt(blend * blend + soft_width * soft_width)
        agree = jnp.where((step > 0.0) == (w > 0.0), jnp.abs(step), 0.0)
        new_w[at, :] = (w - learn_rate * (step + decay_rate * agree * w)).astype(bf16)
        new_m[at, :] = blend.astype(bf16)


def down(cap, sizes, ndp, dp_idx, pieces, blocks, wd, mom, deps):
    h, s = wd.shape
    hq = h // ndp
    rows = cap * sum(sizes)
    col = pl.BlockSpec((h, TILE), lambda c, i: (0, c))
    return call(
        functools.partial(down_body, cap, sizes, ndp),
        [dp_idx, *pieces, *blocks, wd, mom],
        deps,
        [jax.ShapeDtypeStruct((h, s), bf16)] * 2,
        [whole((p.shape[0], hq)) for p in pieces]
        + [pl.BlockSpec((cap, TILE), lambda c, i: (0, s // TILE + c))] * len(blocks)
        + [col, col],
        [col, col],
        grid=(s // TILE,),
        scalars=1,
        scratch=[pltpu.VMEM((h, rows), bf16), pltpu.VMEM((rows, TILE), bf16)],
    )


def combine_body(cap, offs, chained, me_ref, tgt_ref, *refs):
    nb = len(offs)
    backs = refs[:nb]
    prev = refs[nb] if chained else None
    out, pick_t, rows = refs[-3:]

    @pl.when(pl.program_id(0) == 0)
    def _():
        target = tgt_ref[...]
        slots = lax.broadcasted_iota(jnp.int32, (cap, target.shape[1]), 0)
        for i, k in enumerate(offs):
            hit = jnp.where(slots + (me_ref[0] ^ k) * cap == target, 1.0, 0.0)
            pick_t[i * cap : (i + 1) * cap, :] = hit.astype(bf16)

    for i, blk in enumerate(backs):
        rows[i * cap : (i + 1) * cap, :] = blk[...]
    total = dot(pick_t[...], rows[...], 0, 0)
    if chained:
        total = total + prev[...].astype(f32)
    out[...] = total.astype(bf16)


def combine(cap, offs, me, target, backs, prev, deps):
    t = target.shape[1]
    s = backs[0].shape[1]
    nb = len(offs)
    col = pl.BlockSpec((t, TILE), lambda c, i: (0, c))
    extra = [] if prev is None else [prev]
    return call(
        functools.partial(combine_body, cap, offs, prev is not None),
        [me, target, *backs, *extra],
        deps,
        jax.ShapeDtypeStruct((t, s), bf16),
        [whole((1, t))] + [pl.BlockSpec((cap, TILE), lambda c, i: (0, c))] * nb + [col] * len(extra),
        col,
        grid=(s // TILE,),
        scalars=1,
        scratch=[pltpu.VMEM((nb * cap, t), bf16), pltpu.VMEM((nb * cap, TILE), bf16)],
    )


def local(tokens, grad_out, route_ids, gate_codes, gate_weight, up_weight, down_weight, momentum):
    n = lax.axis_size("expert")
    ndp = lax.axis_size("dp")
    t = tokens.shape[0]
    most = max(2, t * 5 // (4 * n))
    cap = -(-most // 16) * 16
    me = lax.axis_index("expert").astype(jnp.int32).reshape(1)
    dp_idx = lax.axis_index("dp").astype(jnp.int32).reshape(1)
    ids = route_ids.reshape(1, t)
    codes = gate_codes.reshape(1, t)
    wg, wu, wd, mom = gate_weight[0], up_weight[0], down_weight[0], momentum[0]

    def swap_expert(v, k):
        return lax.ppermute(v, "expert", [(i, i ^ k) for i in range(n)])

    def swap_dp(v, k):
        return lax.ppermute(v, "dp", [(i, i ^ k) for i in range(ndp)])

    far, near = grouping(n)
    chunks = [near[0], near[1] + far[0], near[2] + far[1], far[2], far[3]]
    send, got, ready, back, pieces, parts = {}, {}, {}, {}, {}, {}
    mark = []

    def push(offs, deps):
        for k in offs:
            if deps:
                send[k] = after(send[k], mark + deps)
                mark[:] = [send[k]]
            got[k] = swap_expert(send[k], k) if k else send[k]

    def give_back(offs, deps):
        for k in offs:
            rows = ready[k]
            if deps:
                rows = after(rows, mark + deps)
                mark[:] = [rows]
            back[k] = swap_expert(rows, k) if k else rows

    def fwd(c):
        own, *others = forward(cap, ndp, dp_idx, [got[k] for k in chunks[c]], wg, wu, wd, mark)
        mark[:] = [own]
        parts[c] = [own] + [swap_dp(v, d + 1) for d, v in enumerate(others)]

    def act(c):
        own = activate(parts[c], mark)
        mark[:] = [own]
        pieces[c] = [own] + [swap_dp(own, d) for d in range(1, ndp)]

    def bwd(c):
        rows = backward(cap, len(chunks[c]), ndp, dp_idx, pieces[c], wg, wu, mark)
        mark[:] = [rows[0]]
        ready.update(zip(chunks[c], rows))

    def gotten(offs):
        return [got[k] for k in offs]

    target, *sends = dispatch(n, cap, far[0], me, ids, codes, tokens, grad_out, True, [])
    send.update(zip(far[0], sends))
    mark[:] = [sends[0]]
    push(far[0], [])
    for offs in (near[0], near[1], far[1] + near[2], far[2] + far[3]):
        sends = dispatch(n, cap, offs, me, target, codes, tokens, grad_out, False, mark)
        send.update(zip(offs, sends))
        mark[:] = [sends[0]]
        if offs in near:
            push(offs, [])

    fwd(0)
    act(0)
    push(far[1], gotten(far[0]))
    push(near[2], gotten(near[1]))
    fwd(1)
    bwd(0)
    give_back(near[0], [])
    act(1)
    push(far[2], gotten(far[1]))
    fwd(2)
    bwd(1)
    act(2)
    push(far[3], gotten(far[2]))
    fwd(3)
    bwd(2)
    act(3)
    give_back(far[0] + near[1], gotten(far[3]))
    fwd(4)
    bwd(3)
    act(4)
    give_back(far[1] + near[2], [back[k] for k in far[0] + near[1]])
    bwd(4)
    give_back(far[2], [back[k] for k in far[1]])
    give_back(far[3], [])
    order = range(len(chunks))
    flat = [k for c in order for k in chunks[c]]
    new_down, new_moment = down(
        cap,
        [len(chunks[c]) for c in order],
        ndp,
        dp_idx,
        [p for c in order for p in pieces[c]],
        gotten(flat),
        wd,
        mom,
        mark,
    )
    mark[:] = [new_down]
    tail = far[2] + far[3]
    early = [k for k in flat if k not in tail]
    part = combine(cap, early, me, target, [back[k] for k in early], None, mark)
    grad_tokens = combine(cap, tail, me, target, [back[k] for k in tail], part, [])
    return (grad_tokens, new_down[None], new_moment[None])


def solution(mesh):
    placed = (
        P("expert", "dp"),
        P("expert", "dp"),
        P("expert", None),
        P("expert", None),
        P("expert", "dp", None),
        P("expert", "dp", None),
        P("expert", None, "dp"),
        P("expert", None, "dp"),
    )
    return jax.shard_map(
        local,
        mesh=mesh,
        in_specs=placed,
        out_specs=(P("expert", "dp"), P("expert", None, "dp"), P("expert", None, "dp")),
        check_vma=False,
    )
```

```python
import functools

import jax
import jax.numpy as jnp
from jax import lax
from jax.experimental import pallas as pl
from jax.experimental.pallas import tpu as pltpu
from jax.sharding import PartitionSpec as P

first_beta = 0.9
learn_rate = 0.01
decay_rate = 3.0
soft_width = 1.0

TILE = 256
VMEM_BYTES = 24 * 1024 * 1024

bf16 = jnp.bfloat16
f32 = jnp.float32


def grouping(n):
    half = n // 2
    step = max(1, half // 4)
    far = [list(range(i, i + step)) for i in range(half, n, step)]
    cuts = [0, half - 2 * step, half - step, half]
    return far, [list(range(i, j)) for i, j in zip(cuts, cuts[1:])]


def skipping(body, n_in, n_deps):
    def run(*refs):
        body(*refs[:n_in], *refs[n_in + n_deps :])

    return run


def call(body, operands, deps, out_shape, in_specs, out_specs, grid=(), scalars=0, scratch=(), aliases=None):
    any_spec = pl.BlockSpec(memory_space=pl.ANY)
    return pl.pallas_call(
        skipping(body, len(operands), len(deps)),
        out_shape=out_shape,
        grid_spec=pltpu.PrefetchScalarGridSpec(
            num_scalar_prefetch=scalars,
            grid=grid,
            in_specs=list(in_specs) + [any_spec] * len(deps),
            out_specs=out_specs,
            scratch_shapes=list(scratch),
        ),
        input_output_aliases=aliases or {},
        compiler_params=pltpu.CompilerParams(vmem_limit_bytes=VMEM_BYTES),
        cost_estimate=pl.CostEstimate(flops=0, bytes_accessed=0, transcendentals=0),
    )(*operands, *deps)


def dot(a, b, ca=1, cb=0):
    return lax.dot_general(a, b, (((ca,), (cb,)), ((), ())), preferred_element_type=f32)


def whole(shape):
    return pl.BlockSpec(shape, lambda *_: (0,) * len(shape))


def after_body(*refs):
    pass


def after(value, deps):
    any_spec = pl.BlockSpec(memory_space=pl.ANY)
    return call(
        after_body, [value], deps, jax.ShapeDtypeStruct(value.shape, value.dtype), [any_spec], any_spec, aliases={0: 0}
    )


def dispatch_body(n, cap, offs, first, *refs):
    if first:
        me_ref, ids_ref, codes_ref, x_ref, g_ref, target_ref, *outs = refs
        ids = ids_ref[...]
        t = ids.shape[1]
        hot = (lax.broadcasted_iota(jnp.int32, (n, t), 0) == ids).astype(f32)
        before = (
            lax.broadcasted_iota(jnp.int32, (t, t), 0) < lax.broadcasted_iota(jnp.int32, (t, t), 1)
        ).astype(f32)
        counts = dot(hot.astype(bf16), before.astype(bf16))
        rank = jnp.sum(hot * counts, axis=0, keepdims=True).astype(jnp.int32)
        target = ids * cap + rank
        target_ref[...] = target
    else:
        me_ref, tgt_ref, codes_ref, x_ref, g_ref, *outs = refs
        target = tgt_ref[...]
    t, s = x_ref.shape
    scale = codes_ref[...].astype(f32) / 256.0
    slots = lax.broadcasted_iota(jnp.int32, (cap, t), 0)
    hits = [slots + (me_ref[0] ^ k) * cap == target for k in offs]
    pick = jnp.concatenate([jnp.where(h, 1.0, 0.0).astype(bf16) for h in hits], axis=0)
    scaled = jnp.concatenate([jnp.where(h, scale, 0.0).astype(bf16) for h in hits], axis=0)
    for c in range(0, s, TILE):
        for left, ref, base in ((pick, x_ref, 0), (scaled, g_ref, s)):
            rows = dot(left, ref[:, c : c + TILE]).astype(bf16)
            for i, out in enumerate(outs):
                out[:, base + c : base + c + TILE] = rows[i * cap : (i + 1) * cap]


def dispatch(n, cap, offs, me, marks, codes, x, g, first, deps):
    t, s = x.shape
    out_shape = [jax.ShapeDtypeStruct((cap, 2 * s), bf16) for _ in offs]
    if first:
        out_shape = [jax.ShapeDtypeStruct((1, t), jnp.int32)] + out_shape
    vmem = pl.BlockSpec(memory_space=pltpu.VMEM)
    return call(
        functools.partial(dispatch_body, n, cap, offs, first),
        [me, marks, codes, x, g],
        deps,
        out_shape,
        [pl.BlockSpec(memory_space=pltpu.SMEM)] + [vmem] * 4,
        [vmem] * len(out_shape),
    )


def forward_body(cap, nb, ndp, dp_ref, *refs):
    blocks, (wg, wu, wd), outs, rows = refs[:nb], refs[nb : nb + 3], refs[nb + 3 : -1], refs[-1]
    d = pl.program_id(0)
    s = wg.shape[0]
    hq = wg.shape[1]

    @pl.when(d == 0)
    def _():
        for i, blk in enumerate(blocks):
            rows[i * cap : (i + 1) * cap, :] = blk[...]

    x = rows[:, :s]
    r = rows[:, s:]
    a = dot(x, wg[...]).astype(bf16)
    b = dot(x, wu[...]).astype(bf16)
    q = dot(r, wd[...], 1, 1).astype(bf16)
    for k in range(ndp):

        @pl.when(d == k)
        def _():
            outs[k][:, :hq] = a
            outs[k][:, hq : 2 * hq] = b
            outs[k][:, 2 * hq :] = q


def forward(cap, ndp, dp_idx, blocks, wg, wu, wd, deps):
    s, h = wg.shape
    hq = h // ndp
    nb = len(blocks)
    rows = nb * cap
    return call(
        functools.partial(forward_body, cap, nb, ndp),
        [dp_idx, *blocks, wg, wu, wd],
        deps,
        [jax.ShapeDtypeStruct((rows, 3 * hq), bf16)] * ndp,
        [whole((cap, 2 * s))] * nb
        + [pl.BlockSpec((s, hq), lambda d, i: (0, i[0] ^ d))] * 2
        + [pl.BlockSpec((hq, s), lambda d, i: (i[0] ^ d, 0))],
        [whole((rows, 3 * hq))] * ndp,
        grid=(ndp,),
        scalars=1,
        scratch=[pltpu.VMEM((rows, 2 * s), bf16)],
    )


def activate_body(*refs):
    *parts, out = refs
    hq = out.shape[1] // 3

    def total(j):
        t = parts[0][:, j * hq : (j + 1) * hq].astype(f32)
        for p in parts[1:]:
            t = t + p[:, j * hq : (j + 1) * hq].astype(f32)
        return t

    a, b, q = total(0), total(1), total(2)
    sigma = jax.nn.sigmoid(a)
    act = a * sigma
    out[:, :hq] = (act * b).astype(bf16)
    out[:, hq : 2 * hq] = (q * b * sigma * (1.0 + a * (1.0 - sigma))).astype(bf16)
    out[:, 2 * hq :] = (q * act).astype(bf16)


def activate(parts, deps):
    vmem = pl.BlockSpec(memory_space=pltpu.VMEM)
    return call(
        activate_body, parts, deps, jax.ShapeDtypeStruct(parts[0].shape, bf16), [vmem] * len(parts), vmem
    )


def backward_body(cap, nb, ndp, dp_ref, *refs):
    pieces, (wg, wu), outs, (dg, du) = refs[:ndp], refs[ndp : ndp + 2], refs[ndp + 2 : -2], refs[-2:]
    hq = pieces[0].shape[1] // 3

    @pl.when(pl.program_id(0) == 0)
    def _():
        for d, piece in enumerate(pieces):
            at = pl.ds(pl.multiple_of((dp_ref[0] ^ d) * hq, hq), hq)
            dg[:, at] = piece[:, hq : 2 * hq]
            du[:, at] = piece[:, 2 * hq :]

    rows = (dot(dg[...], wg[...], 1, 1) + dot(du[...], wu[...], 1, 1)).astype(bf16)
    for i, out in enumerate(outs):
        out[...] = rows[i * cap : (i + 1) * cap]


def backward(cap, nb, ndp, dp_idx, pieces, wg, wu, deps):
    s, h = wg.shape
    return call(
        functools.partial(backward_body, cap, nb, ndp),
        [dp_idx, *pieces, wg, wu],
        deps,
        [jax.ShapeDtypeStruct((cap, s), bf16)] * nb,
        [whole(pieces[0].shape)] * ndp + [pl.BlockSpec((TILE, h), lambda c, i: (c, 0))] * 2,
        [pl.BlockSpec((cap, TILE), lambda c, i: (0, c))] * nb,
        grid=(s // TILE,),
        scalars=1,
        scratch=[pltpu.VMEM((nb * cap, h), bf16)] * 2,
    )


def down_body(cap, sizes, ndp, dp_ref, *refs):
    n_pieces = len(sizes) * ndp
    n_blocks = sum(sizes)
    pieces = refs[:n_pieces]
    blocks = refs[n_pieces : n_pieces + n_blocks]
    wd, mom, new_w, new_m, token, hid_t, dy = refs[n_pieces + n_blocks :]
    hq = pieces[0].shape[1]

    @pl.when(pl.program_id(0) == 0)
    def _():
        token[...] = jnp.zeros_like(token)
        base = 0
        for g, size in enumerate(sizes):
            for d in range(ndp):
                at = pl.ds(pl.multiple_of((dp_ref[0] ^ d) * hq, hq), hq)
                piece = pieces[g * ndp + d][...].astype(f32)
                hid_t[at, base : base + size * cap] = piece.T.astype(bf16)
            base += size * cap

    for i, blk in enumerate(blocks):
        dy[i * cap : (i + 1) * cap, :] = blk[...]
    step_rows = 128
    for c in range(0, hid_t.shape[0], step_rows):
        at = slice(c, c + step_rows)
        grad = dot(hid_t[at, :], dy[...])
        w = wd[at, :].astype(f32)
        blend = first_beta * mom[at, :].astype(f32) + (1.0 - first_beta) * grad
        step = blend * lax.rsqrt(blend * blend + soft_width * soft_width)
        agree = jnp.where((step > 0.0) == (w > 0.0), jnp.abs(step), 0.0)
        new_w[at, :] = (w - learn_rate * (step + decay_rate * agree * w)).astype(bf16)
        new_m[at, :] = blend.astype(bf16)


def down(cap, sizes, ndp, dp_idx, pieces, blocks, wd, mom, deps):
    h, s = wd.shape
    hq = h // ndp
    rows = cap * sum(sizes)
    col = pl.BlockSpec((h, TILE), lambda c, i: (0, c))
    return call(
        functools.partial(down_body, cap, sizes, ndp),
        [dp_idx, *pieces, *blocks, wd, mom],
        deps,
        [jax.ShapeDtypeStruct((h, s), bf16)] * 2 + [jax.ShapeDtypeStruct((8, 128), f32)],
        [whole((p.shape[0], hq)) for p in pieces]
        + [pl.BlockSpec((cap, TILE), lambda c, i: (0, s // TILE + c))] * len(blocks)
        + [col, col],
        [col, col, whole((8, 128))],
        grid=(s // TILE,),
        scalars=1,
        scratch=[pltpu.VMEM((h, rows), bf16), pltpu.VMEM((rows, TILE), bf16)],
    )


def combine_body(cap, offs, chained, me_ref, tgt_ref, *refs):
    nb = len(offs)
    backs = refs[:nb]
    prev = refs[nb] if chained else None
    out, pick_t, rows = refs[-3:]

    @pl.when(pl.program_id(0) == 0)
    def _():
        target = tgt_ref[...]
        slots = lax.broadcasted_iota(jnp.int32, (cap, target.shape[1]), 0)
        for i, k in enumerate(offs):
            hit = jnp.where(slots + (me_ref[0] ^ k) * cap == target, 1.0, 0.0)
            pick_t[i * cap : (i + 1) * cap, :] = hit.astype(bf16)

    for i, blk in enumerate(backs):
        rows[i * cap : (i + 1) * cap, :] = blk[...]
    total = dot(pick_t[...], rows[...], 0, 0)
    if chained:
        total = total + prev[...].astype(f32)
    out[...] = total.astype(bf16)


def combine(cap, offs, me, target, backs, prev, deps):
    t = target.shape[1]
    s = backs[0].shape[1]
    nb = len(offs)
    col = pl.BlockSpec((t, TILE), lambda c, i: (0, c))
    extra = [] if prev is None else [prev]
    return call(
        functools.partial(combine_body, cap, offs, prev is not None),
        [me, target, *backs, *extra],
        deps,
        jax.ShapeDtypeStruct((t, s), bf16),
        [whole((1, t))] + [pl.BlockSpec((cap, TILE), lambda c, i: (0, c))] * nb + [col] * len(extra),
        col,
        grid=(s // TILE,),
        scalars=1,
        scratch=[pltpu.VMEM((nb * cap, t), bf16), pltpu.VMEM((nb * cap, TILE), bf16)],
    )


def local(tokens, grad_out, route_ids, gate_codes, gate_weight, up_weight, down_weight, momentum):
    n = lax.axis_size("expert")
    ndp = lax.axis_size("dp")
    t = tokens.shape[0]
    most = max(2, t * 5 // (4 * n))
    cap = -(-most // 16) * 16
    me = lax.axis_index("expert").astype(jnp.int32).reshape(1)
    dp_idx = lax.axis_index("dp").astype(jnp.int32).reshape(1)
    ids = route_ids.reshape(1, t)
    codes = gate_codes.reshape(1, t)
    wg, wu, wd, mom = gate_weight[0], up_weight[0], down_weight[0], momentum[0]

    def swap_expert(v, k):
        return lax.ppermute(v, "expert", [(i, i ^ k) for i in range(n)])

    def swap_dp(v, k):
        return lax.ppermute(v, "dp", [(i, i ^ k) for i in range(ndp)])

    far, near = grouping(n)
    chunks = [near[0], far[0], far[1] + near[1], far[2] + near[2], far[3]]
    send, got, ready, back, pieces, parts = {}, {}, {}, {}, {}, {}
    mark = []

    def push(offs, deps):
        for k in offs:
            if deps:
                send[k] = after(send[k], mark + deps)
                mark[:] = [send[k]]
            got[k] = swap_expert(send[k], k) if k else send[k]

    def give_back(offs, deps):
        for k in offs:
            rows = ready[k]
            if deps:
                rows = after(rows, mark + deps)
                mark[:] = [rows]
            back[k] = swap_expert(rows, k) if k else rows

    def fwd(c):
        own, *others = forward(cap, ndp, dp_idx, [got[k] for k in chunks[c]], wg, wu, wd, mark)
        mark[:] = [own]
        parts[c] = [own] + [swap_dp(v, d + 1) for d, v in enumerate(others)]

    def act(c):
        own = activate(parts[c], mark)
        mark[:] = [own]
        pieces[c] = [own] + [swap_dp(own, d) for d in range(1, ndp)]

    def bwd(c):
        rows = backward(cap, len(chunks[c]), ndp, dp_idx, pieces[c], wg, wu, mark)
        mark[:] = [rows[0]]
        ready.update(zip(chunks[c], rows))

    def gotten(offs):
        return [got[k] for k in offs]

    offs = far[0] + near[0]
    target, *sends = dispatch(n, cap, offs, me, ids, codes, tokens, grad_out, True, [])
    send.update(zip(offs, sends))
    mark[:] = [sends[0]]
    push(offs, [])
    offs = far[1] + near[1] + far[2] + near[2] + far[3]
    sends = dispatch(n, cap, offs, me, target, codes, tokens, grad_out, False, mark)
    send.update(zip(offs, sends))
    mark[:] = [sends[0]]

    fwd(0)
    push(far[1] + near[1], gotten(far[0]))
    act(0)
    fwd(1)
    bwd(0)
    act(1)
    push(far[2] + near[2], gotten(far[1] + near[1]))
    give_back(near[0], [])
    fwd(2)
    bwd(1)
    act(2)
    push(far[3], gotten(far[2] + near[2]))
    fwd(3)
    bwd(2)
    give_back(near[1], [])
    act(3)
    give_back(far[0], gotten(far[3]) + [back[k] for k in near[1] + near[0][1:]])
    give_back(far[1], [])
    fwd(4)
    bwd(3)
    act(4)
    give_back(far[2], [back[k] for k in far[0]])
    give_back(near[2], [])
    bwd(4)
    give_back(far[3], [])
    order = range(len(chunks))
    flat = [k for c in order for k in chunks[c]]
    new_down, new_moment, token = down(
        cap,
        [len(chunks[c]) for c in order],
        ndp,
        dp_idx,
        [p for c in order for p in pieces[c]],
        gotten(flat),
        wd,
        mom,
        mark,
    )
    mark[:] = [token]
    tail = far[2] + far[3]
    early = [k for k in flat if k not in tail]
    part = combine(cap, early, me, target, [back[k] for k in early], None, mark)
    grad_tokens = combine(cap, tail, me, target, [back[k] for k in tail], part, [])
    return (grad_tokens, new_down[None], new_moment[None])


def solution(mesh):
    placed = (
        P("expert", "dp"),
        P("expert", "dp"),
        P("expert", None),
        P("expert", None),
        P("expert", "dp", None),
        P("expert", "dp", None),
        P("expert", None, "dp"),
        P("expert", None, "dp"),
    )
    return jax.shard_map(
        local,
        mesh=mesh,
        in_specs=placed,
        out_specs=(P("expert", "dp"), P("expert", None, "dp"), P("expert", None, "dp")),
        check_vma=False,
    )
```

```python
import functools

import jax
import jax.numpy as jnp
from jax import lax
from jax.experimental import pallas as pl
from jax.experimental.pallas import tpu as pltpu
from jax.sharding import PartitionSpec as P

first_beta = 0.9
learn_rate = 0.01
decay_rate = 3.0
soft_width = 1.0

TILE = 256
VMEM_BYTES = 24 * 1024 * 1024
LEAD_BYTES = 60 * 1024 * 1024

bf16 = jnp.bfloat16
f32 = jnp.float32


def grouping(n):
    half = n // 2
    step = max(1, half // 4)
    far = [list(range(i, i + step)) for i in range(half, n, step)]
    cuts = [0, half - 2 * step, half - step, half]
    return far, [list(range(i, j)) for i, j in zip(cuts, cuts[1:])]


def skipping(body, n_in, n_deps):
    def run(*refs):
        body(*refs[:n_in], *refs[n_in + n_deps :])

    return run


def call(body, operands, deps, out_shape, in_specs, out_specs, grid=(), scalars=0, scratch=(), aliases=None, limit=VMEM_BYTES):
    any_spec = pl.BlockSpec(memory_space=pl.ANY)
    return pl.pallas_call(
        skipping(body, len(operands), len(deps)),
        out_shape=out_shape,
        grid_spec=pltpu.PrefetchScalarGridSpec(
            num_scalar_prefetch=scalars,
            grid=grid,
            in_specs=list(in_specs) + [any_spec] * len(deps),
            out_specs=out_specs,
            scratch_shapes=list(scratch),
        ),
        input_output_aliases=aliases or {},
        compiler_params=pltpu.CompilerParams(vmem_limit_bytes=limit),
        cost_estimate=pl.CostEstimate(flops=0, bytes_accessed=0, transcendentals=0),
    )(*operands, *deps)


def dot(a, b, ca=1, cb=0):
    return lax.dot_general(a, b, (((ca,), (cb,)), ((), ())), preferred_element_type=f32)


def whole(shape):
    return pl.BlockSpec(shape, lambda *_: (0,) * len(shape))


def after_body(*refs):
    pass


def after(value, deps):
    any_spec = pl.BlockSpec(memory_space=pl.ANY)
    return call(
        after_body, [value], deps, jax.ShapeDtypeStruct(value.shape, value.dtype), [any_spec], any_spec, aliases={0: 0}
    )


def picks(cap, offs, me, target, scale):
    slots = lax.broadcasted_iota(jnp.int32, (cap, target.shape[1]), 0)
    hits = [slots + (me ^ k) * cap == target for k in offs]
    pick = jnp.concatenate([jnp.where(h, 1.0, 0.0).astype(bf16) for h in hits], axis=0)
    scaled = jnp.concatenate([jnp.where(h, scale, 0.0).astype(bf16) for h in hits], axis=0)
    return pick, scaled


def dispatch_body(n, cap, offs, cuts, me_ref, ids_ref, codes_ref, x_ref, g_ref, target_ref, *refs):
    *outs, ids_v, codes_v, x_v, g_v, sems = refs
    small = [
        pltpu.make_async_copy(ids_ref, ids_v, sems.at[0]),
        pltpu.make_async_copy(codes_ref, codes_v, sems.at[1]),
    ]
    large = []
    for c0, c1 in cuts:
        for ref, buf in ((x_ref, x_v), (g_ref, g_v)):
            large.append(pltpu.make_async_copy(ref.at[:, c0:c1], buf.at[:, c0:c1], sems.at[2 + len(large)]))
    for copy in small + large:
        copy.start()
    small[0].wait()
    ids = ids_v[...]
    t, s = x_v.shape
    hot = (lax.broadcasted_iota(jnp.int32, (n, t), 0) == ids).astype(f32)
    before = (
        lax.broadcasted_iota(jnp.int32, (t, t), 0) < lax.broadcasted_iota(jnp.int32, (t, t), 1)
    ).astype(f32)
    counts = dot(hot.astype(bf16), before.astype(bf16))
    rank = jnp.sum(hot * counts, axis=0, keepdims=True).astype(jnp.int32)
    target = ids * cap + rank
    target_ref[...] = target
    small[1].wait()
    pick, scaled = picks(cap, offs, me_ref[0], target, codes_v[...].astype(f32) / 256.0)
    for j, (c0, c1) in enumerate(cuts):
        for which, (left, buf, base) in enumerate(((pick, x_v, 0), (scaled, g_v, s))):
            large[2 * j + which].wait()
            for c in range(c0, c1, TILE):
                rows = dot(left, buf[:, c : c + TILE]).astype(bf16)
                for i, out in enumerate(outs):
                    out[:, base + c : base + c + TILE] = rows[i * cap : (i + 1) * cap]


def dispatch(n, cap, offs, me, ids, codes, x, g, deps):
    t, s = x.shape
    half = s // (2 * TILE) * TILE
    cuts = [(0, half), (half, s)]
    out_shape = [jax.ShapeDtypeStruct((1, t), jnp.int32)] + [jax.ShapeDtypeStruct((cap, 2 * s), bf16) for _ in offs]
    far_memory = pl.BlockSpec(memory_space=pltpu.HBM)
    return call(
        functools.partial(dispatch_body, n, cap, offs, cuts),
        [me, ids, codes, x, g],
        deps,
        out_shape,
        [pl.BlockSpec(memory_space=pltpu.SMEM)] + [far_memory] * 4,
        [pl.BlockSpec(memory_space=pltpu.VMEM)] * len(out_shape),
        scratch=[
            pltpu.VMEM((1, t), jnp.int32),
            pltpu.VMEM((1, t), jnp.int32),
            pltpu.VMEM((t, s), bf16),
            pltpu.VMEM((t, s), bf16),
            pltpu.SemaphoreType.DMA((2 + 2 * len(cuts),)),
        ],
        limit=LEAD_BYTES,
    )


def forward_body(cap, nb, ndp, dp_ref, *refs):
    blocks, (wg, wu, wd), outs, rows = refs[:nb], refs[nb : nb + 3], refs[nb + 3 : -1], refs[-1]
    d = pl.program_id(0)
    s = wg.shape[0]
    hq = wg.shape[1]

    @pl.when(d == 0)
    def _():
        for i, blk in enumerate(blocks):
            rows[i * cap : (i + 1) * cap, :] = blk[...]

    x = rows[:, :s]
    r = rows[:, s:]
    a = dot(x, wg[...]).astype(bf16)
    b = dot(x, wu[...]).astype(bf16)
    q = dot(r, wd[...], 1, 1).astype(bf16)
    for k in range(ndp):

        @pl.when(d == k)
        def _():
            outs[k][:, :hq] = a
            outs[k][:, hq : 2 * hq] = b
            outs[k][:, 2 * hq :] = q


def forward(cap, ndp, dp_idx, blocks, wg, wu, wd, deps):
    s, h = wg.shape
    hq = h // ndp
    nb = len(blocks)
    rows = nb * cap
    return call(
        functools.partial(forward_body, cap, nb, ndp),
        [dp_idx, *blocks, wg, wu, wd],
        deps,
        [jax.ShapeDtypeStruct((rows, 3 * hq), bf16)] * ndp,
        [whole((cap, 2 * s))] * nb
        + [pl.BlockSpec((s, hq), lambda d, i: (0, i[0] ^ d))] * 2
        + [pl.BlockSpec((hq, s), lambda d, i: (i[0] ^ d, 0))],
        [whole((rows, 3 * hq))] * ndp,
        grid=(ndp,),
        scalars=1,
        scratch=[pltpu.VMEM((rows, 2 * s), bf16)],
    )


def activate_body(*refs):
    *parts, out = refs
    hq = out.shape[1] // 3

    def total(j):
        t = parts[0][:, j * hq : (j + 1) * hq].astype(f32)
        for p in parts[1:]:
            t = t + p[:, j * hq : (j + 1) * hq].astype(f32)
        return t

    a, b, q = total(0), total(1), total(2)
    sigma = jax.nn.sigmoid(a)
    act = a * sigma
    out[:, :hq] = (act * b).astype(bf16)
    out[:, hq : 2 * hq] = (q * b * sigma * (1.0 + a * (1.0 - sigma))).astype(bf16)
    out[:, 2 * hq :] = (q * act).astype(bf16)


def activate(parts, deps):
    vmem = pl.BlockSpec(memory_space=pltpu.VMEM)
    return call(
        activate_body, parts, deps, jax.ShapeDtypeStruct(parts[0].shape, bf16), [vmem] * len(parts), vmem
    )


def backward_body(cap, nb, ndp, dp_ref, *refs):
    pieces, (wg, wu), outs, (dg, du) = refs[:ndp], refs[ndp : ndp + 2], refs[ndp + 2 : -2], refs[-2:]
    hq = pieces[0].shape[1] // 3

    @pl.when(pl.program_id(0) == 0)
    def _():
        for d, piece in enumerate(pieces):
            at = pl.ds(pl.multiple_of((dp_ref[0] ^ d) * hq, hq), hq)
            dg[:, at] = piece[:, hq : 2 * hq]
            du[:, at] = piece[:, 2 * hq :]

    rows = (dot(dg[...], wg[...], 1, 1) + dot(du[...], wu[...], 1, 1)).astype(bf16)
    for i, out in enumerate(outs):
        out[...] = rows[i * cap : (i + 1) * cap]


def backward(cap, nb, ndp, dp_idx, pieces, wg, wu, deps):
    s, h = wg.shape
    return call(
        functools.partial(backward_body, cap, nb, ndp),
        [dp_idx, *pieces, wg, wu],
        deps,
        [jax.ShapeDtypeStruct((cap, s), bf16)] * nb,
        [whole(pieces[0].shape)] * ndp + [pl.BlockSpec((TILE, h), lambda c, i: (c, 0))] * 2,
        [pl.BlockSpec((cap, TILE), lambda c, i: (0, c))] * nb,
        grid=(s // TILE,),
        scalars=1,
        scratch=[pltpu.VMEM((nb * cap, h), bf16)] * 2,
    )


def down_body(cap, sizes, ndp, dp_ref, *refs):
    n_pieces = len(sizes) * ndp
    n_blocks = sum(sizes)
    pieces = refs[:n_pieces]
    blocks = refs[n_pieces : n_pieces + n_blocks]
    wd, mom, new_w, new_m, token, hid_t, dy = refs[n_pieces + n_blocks :]
    hq = pieces[0].shape[1]

    @pl.when(pl.program_id(0) == 0)
    def _():
        token[...] = jnp.zeros_like(token)
        base = 0
        for g, size in enumerate(sizes):
            for d in range(ndp):
                at = pl.ds(pl.multiple_of((dp_ref[0] ^ d) * hq, hq), hq)
                piece = pieces[g * ndp + d][...].astype(f32)
                hid_t[at, base : base + size * cap] = piece.T.astype(bf16)
            base += size * cap

    for i, blk in enumerate(blocks):
        dy[i * cap : (i + 1) * cap, :] = blk[...]
    step_rows = 128
    for c in range(0, hid_t.shape[0], step_rows):
        at = slice(c, c + step_rows)
        grad = dot(hid_t[at, :], dy[...])
        w = wd[at, :].astype(f32)
        blend = first_beta * mom[at, :].astype(f32) + (1.0 - first_beta) * grad
        step = blend * lax.rsqrt(blend * blend + soft_width * soft_width)
        agree = jnp.where((step > 0.0) == (w > 0.0), jnp.abs(step), 0.0)
        new_w[at, :] = (w - learn_rate * (step + decay_rate * agree * w)).astype(bf16)
        new_m[at, :] = blend.astype(bf16)


def down(cap, sizes, ndp, dp_idx, pieces, blocks, wd, mom, deps):
    h, s = wd.shape
    hq = h // ndp
    rows = cap * sum(sizes)
    col = pl.BlockSpec((h, TILE), lambda c, i: (0, c))
    return call(
        functools.partial(down_body, cap, sizes, ndp),
        [dp_idx, *pieces, *blocks, wd, mom],
        deps,
        [jax.ShapeDtypeStruct((h, s), bf16)] * 2 + [jax.ShapeDtypeStruct((8, 128), f32)],
        [whole((p.shape[0], hq)) for p in pieces]
        + [pl.BlockSpec((cap, TILE), lambda c, i: (0, s // TILE + c))] * len(blocks)
        + [col, col],
        [col, col, whole((8, 128))],
        grid=(s // TILE,),
        scalars=1,
        scratch=[pltpu.VMEM((h, rows), bf16), pltpu.VMEM((rows, TILE), bf16)],
    )


def combine_body(cap, offs, chained, me_ref, tgt_ref, *refs):
    nb = len(offs)
    backs = refs[:nb]
    prev = refs[nb] if chained else None
    out, pick_t, rows = refs[-3:]

    @pl.when(pl.program_id(0) == 0)
    def _():
        target = tgt_ref[...]
        slots = lax.broadcasted_iota(jnp.int32, (cap, target.shape[1]), 0)
        hits = [jnp.where(slots + (me_ref[0] ^ k) * cap == target, 1.0, 0.0) for k in offs]
        pick_t[...] = jnp.concatenate(hits, axis=0).T.astype(bf16)

    for i, blk in enumerate(backs):
        rows[i * cap : (i + 1) * cap, :] = blk[...]
    total = dot(pick_t[...], rows[...])
    if chained:
        total = total + prev[...].astype(f32)
    out[...] = total.astype(bf16)


def combine(cap, offs, me, target, backs, prev, deps):
    t = target.shape[1]
    s = backs[0].shape[1]
    nb = len(offs)
    wide = s // 2
    col = pl.BlockSpec((t, wide), lambda c, i: (0, c))
    extra = [] if prev is None else [prev]
    return call(
        functools.partial(combine_body, cap, offs, prev is not None),
        [me, target, *backs, *extra],
        deps,
        jax.ShapeDtypeStruct((t, s), bf16),
        [whole((1, t))] + [pl.BlockSpec((cap, wide), lambda c, i: (0, c))] * nb + [col] * len(extra),
        col,
        grid=(s // wide,),
        scalars=1,
        scratch=[pltpu.VMEM((t, nb * cap), bf16), pltpu.VMEM((nb * cap, wide), bf16)],
    )


def local(tokens, grad_out, route_ids, gate_codes, gate_weight, up_weight, down_weight, momentum):
    n = lax.axis_size("expert")
    ndp = lax.axis_size("dp")
    t = tokens.shape[0]
    most = max(2, t * 5 // (4 * n))
    cap = -(-most // 16) * 16
    me = lax.axis_index("expert").astype(jnp.int32).reshape(1)
    dp_idx = lax.axis_index("dp").astype(jnp.int32).reshape(1)
    ids = route_ids.reshape(1, t)
    codes = gate_codes.reshape(1, t)
    wg, wu, wd, mom = gate_weight[0], up_weight[0], down_weight[0], momentum[0]

    def swap_expert(v, k):
        return lax.ppermute(v, "expert", [(i, i ^ k) for i in range(n)])

    def swap_dp(v, k):
        return lax.ppermute(v, "dp", [(i, i ^ k) for i in range(ndp)])

    far, near = grouping(n)
    chunks = [near[0], far[0], far[1] + near[1], far[2] + near[2], far[3]]
    send, got, ready, back, pieces, parts = {}, {}, {}, {}, {}, {}
    mark = []

    def push(offs, deps):
        for k in offs:
            if deps is not None:
                send[k] = after(send[k], mark + deps)
                mark[:] = [send[k]]
            got[k] = swap_expert(send[k], k) if k else send[k]

    def give_back(offs, deps):
        for k in offs:
            rows = ready[k]
            if deps is not None:
                rows = after(rows, mark + deps)
                mark[:] = [rows]
            back[k] = swap_expert(rows, k) if k else rows

    def fwd(c):
        own, *others = forward(cap, ndp, dp_idx, [got[k] for k in chunks[c]], wg, wu, wd, mark)
        mark[:] = [own]
        parts[c] = [own] + [swap_dp(v, d + 1) for d, v in enumerate(others)]

    def act(c):
        own = activate(parts[c], mark)
        mark[:] = [own]
        pieces[c] = [own] + [swap_dp(own, d) for d in range(1, ndp)]

    def bwd(c):
        rows = backward(cap, len(chunks[c]), ndp, dp_idx, pieces[c], wg, wu, mark)
        mark[:] = [rows[0]]
        ready.update(zip(chunks[c], rows))

    def gotten(offs):
        return [got[k] for k in offs]

    offs = far[0] + near[0]
    target, *sends = dispatch(n, cap, offs, me, ids, codes, tokens, grad_out, [])
    send.update(zip(offs, sends))
    mark[:] = [sends[0]]
    push(offs, None)
    offs = far[1] + near[1] + far[2] + near[2] + far[3]
    _, *sends = dispatch(n, cap, offs, me, ids, codes, tokens, grad_out, mark)
    send.update(zip(offs, sends))
    mark[:] = [sends[0]]

    fwd(0)
    push(far[1], [])
    push(near[1], gotten(far[0]))
    act(0)
    fwd(1)
    bwd(0)
    act(1)
    push(far[2], gotten(near[1]))
    push(near[2], gotten(far[1]))
    give_back(near[0], None)
    fwd(2)
    bwd(1)
    act(2)
    push(far[3], gotten(far[2] + near[2]))
    fwd(3)
    bwd(2)
    give_back(near[1], None)
    act(3)
    give_back(far[0], gotten(far[3]) + [back[k] for k in near[1] + near[0][1:]])
    fwd(4)
    bwd(3)
    give_back(far[1] + far[2], [back[k] for k in far[0]])
    act(4)
    bwd(4)
    give_back(far[3], None)
    give_back(near[2], [])
    order = range(len(chunks))
    flat = [k for c in order for k in chunks[c]]
    new_down, new_moment, token = down(
        cap,
        [len(chunks[c]) for c in order],
        ndp,
        dp_idx,
        [p for c in order for p in pieces[c]],
        gotten(flat),
        wd,
        mom,
        mark,
    )
    mark[:] = [token]
    tail = near[2] + far[3]
    early = [k for k in flat if k not in tail]
    part = combine(cap, early, me, target, [back[k] for k in early], None, mark)
    grad_tokens = combine(cap, tail, me, target, [back[k] for k in tail], part, [])
    return (grad_tokens, new_down[None], new_moment[None])


def solution(mesh):
    placed = (
        P("expert", "dp"),
        P("expert", "dp"),
        P("expert", None),
        P("expert", None),
        P("expert", "dp", None),
        P("expert", "dp", None),
        P("expert", None, "dp"),
        P("expert", None, "dp"),
    )
    return jax.shard_map(
        local,
        mesh=mesh,
        in_specs=placed,
        out_specs=(P("expert", "dp"), P("expert", None, "dp"), P("expert", None, "dp")),
        check_vma=False,
    )
```

```python
import functools

import jax
import jax.numpy as jnp
from jax import lax
from jax.experimental import pallas as pl
from jax.experimental.pallas import tpu as pltpu
from jax.sharding import PartitionSpec as P

first_beta = 0.9
learn_rate = 0.01
decay_rate = 3.0
soft_width = 1.0

TILE = 256
VMEM_BYTES = 24 * 1024 * 1024
LEAD_BYTES = 60 * 1024 * 1024

bf16 = jnp.bfloat16
f32 = jnp.float32


def grouping(n):
    half = n // 2
    step = max(1, half // 4)
    far = [list(range(i, i + step)) for i in range(half, n, step)]
    cuts = [0, half - 2 * step, half - step, half]
    return far, [list(range(i, j)) for i, j in zip(cuts, cuts[1:])]


def skipping(body, n_in, n_deps):
    def run(*refs):
        body(*refs[:n_in], *refs[n_in + n_deps :])

    return run


def call(body, operands, deps, out_shape, in_specs, out_specs, grid=(), scalars=0, scratch=(), aliases=None, limit=VMEM_BYTES):
    any_spec = pl.BlockSpec(memory_space=pl.ANY)
    return pl.pallas_call(
        skipping(body, len(operands), len(deps)),
        out_shape=out_shape,
        grid_spec=pltpu.PrefetchScalarGridSpec(
            num_scalar_prefetch=scalars,
            grid=grid,
            in_specs=list(in_specs) + [any_spec] * len(deps),
            out_specs=out_specs,
            scratch_shapes=list(scratch),
        ),
        input_output_aliases=aliases or {},
        compiler_params=pltpu.CompilerParams(vmem_limit_bytes=limit),
        cost_estimate=pl.CostEstimate(flops=0, bytes_accessed=0, transcendentals=0),
    )(*operands, *deps)


def dot(a, b, ca=1, cb=0):
    return lax.dot_general(a, b, (((ca,), (cb,)), ((), ())), preferred_element_type=f32)


def whole(shape):
    return pl.BlockSpec(shape, lambda *_: (0,) * len(shape))


def after_body(*refs):
    pass


def after(value, deps):
    any_spec = pl.BlockSpec(memory_space=pl.ANY)
    return call(
        after_body, [value], deps, jax.ShapeDtypeStruct(value.shape, value.dtype), [any_spec], any_spec, aliases={0: 0}
    )


def picks(cap, offs, me, target, scale):
    slots = lax.broadcasted_iota(jnp.int32, (cap, target.shape[1]), 0)
    hits = [slots + (me ^ k) * cap == target for k in offs]
    pick = jnp.concatenate([jnp.where(h, 1.0, 0.0).astype(bf16) for h in hits], axis=0)
    scaled = jnp.concatenate([jnp.where(h, scale, 0.0).astype(bf16) for h in hits], axis=0)
    return pick, scaled


def dispatch_body(n, cap, offs, cuts, me_ref, ids_ref, codes_ref, x_ref, g_ref, target_ref, *refs):
    *outs, ids_v, codes_v, x_v, g_v, sems = refs
    small = [
        pltpu.make_async_copy(ids_ref, ids_v, sems.at[0]),
        pltpu.make_async_copy(codes_ref, codes_v, sems.at[1]),
    ]
    large = []
    for c0, c1 in cuts:
        for ref, buf in ((x_ref, x_v), (g_ref, g_v)):
            large.append(pltpu.make_async_copy(ref.at[:, c0:c1], buf.at[:, c0:c1], sems.at[2 + len(large)]))
    for copy in small + large:
        copy.start()
    small[0].wait()
    ids = ids_v[...]
    t, s = x_v.shape
    hot = (lax.broadcasted_iota(jnp.int32, (n, t), 0) == ids).astype(f32)
    before = (
        lax.broadcasted_iota(jnp.int32, (t, t), 0) < lax.broadcasted_iota(jnp.int32, (t, t), 1)
    ).astype(f32)
    counts = dot(hot.astype(bf16), before.astype(bf16))
    rank = jnp.sum(hot * counts, axis=0, keepdims=True).astype(jnp.int32)
    target = ids * cap + rank
    target_ref[...] = target
    small[1].wait()
    pick, scaled = picks(cap, offs, me_ref[0], target, codes_v[...].astype(f32) / 256.0)
    for j, (c0, c1) in enumerate(cuts):
        for which, (left, buf, base) in enumerate(((pick, x_v, 0), (scaled, g_v, s))):
            large[2 * j + which].wait()
            for c in range(c0, c1, TILE):
                rows = dot(left, buf[:, c : c + TILE]).astype(bf16)
                for i, out in enumerate(outs):
                    out[:, base + c : base + c + TILE] = rows[i * cap : (i + 1) * cap]


def dispatch(n, cap, offs, me, ids, codes, x, g, deps):
    t, s = x.shape
    half = s // (2 * TILE) * TILE
    cuts = [(0, half), (half, s)]
    out_shape = [jax.ShapeDtypeStruct((1, t), jnp.int32)] + [jax.ShapeDtypeStruct((cap, 2 * s), bf16) for _ in offs]
    far_memory = pl.BlockSpec(memory_space=pltpu.HBM)
    return call(
        functools.partial(dispatch_body, n, cap, offs, cuts),
        [me, ids, codes, x, g],
        deps,
        out_shape,
        [pl.BlockSpec(memory_space=pltpu.SMEM)] + [far_memory] * 4,
        [pl.BlockSpec(memory_space=pltpu.VMEM)] * len(out_shape),
        scratch=[
            pltpu.VMEM((1, t), jnp.int32),
            pltpu.VMEM((1, t), jnp.int32),
            pltpu.VMEM((t, s), bf16),
            pltpu.VMEM((t, s), bf16),
            pltpu.SemaphoreType.DMA((2 + 2 * len(cuts),)),
        ],
        limit=LEAD_BYTES,
    )


def join_body(first, second, out):
    cap = first.shape[0]
    out[:cap, :] = first[...]
    out[cap:, :] = second[...]


def join(first, second, deps):
    cap, s = first.shape
    vmem = pl.BlockSpec(memory_space=pltpu.VMEM)
    return call(join_body, [first, second], deps, jax.ShapeDtypeStruct((2 * cap, s), bf16), [vmem] * 2, vmem)


def forward_body(cap, nb, ndp, dp_ref, *refs):
    blocks, (wg, wu, wd), outs, rows = refs[:nb], refs[nb : nb + 3], refs[nb + 3 : -1], refs[-1]
    d = pl.program_id(0)
    s = wg.shape[0]
    hq = wg.shape[1]

    @pl.when(d == 0)
    def _():
        for i, blk in enumerate(blocks):
            rows[i * cap : (i + 1) * cap, :] = blk[...]

    x = rows[:, :s]
    r = rows[:, s:]
    a = dot(x, wg[...]).astype(bf16)
    b = dot(x, wu[...]).astype(bf16)
    q = dot(r, wd[...], 1, 1).astype(bf16)
    for k in range(ndp):

        @pl.when(d == k)
        def _():
            outs[k][:, :hq] = a
            outs[k][:, hq : 2 * hq] = b
            outs[k][:, 2 * hq :] = q


def forward(cap, ndp, dp_idx, blocks, wg, wu, wd, deps):
    s, h = wg.shape
    hq = h // ndp
    nb = len(blocks)
    rows = nb * cap
    return call(
        functools.partial(forward_body, cap, nb, ndp),
        [dp_idx, *blocks, wg, wu, wd],
        deps,
        [jax.ShapeDtypeStruct((rows, 3 * hq), bf16)] * ndp,
        [whole((cap, 2 * s))] * nb
        + [pl.BlockSpec((s, hq), lambda d, i: (0, i[0] ^ d))] * 2
        + [pl.BlockSpec((hq, s), lambda d, i: (i[0] ^ d, 0))],
        [whole((rows, 3 * hq))] * ndp,
        grid=(ndp,),
        scalars=1,
        scratch=[pltpu.VMEM((rows, 2 * s), bf16)],
    )


def activate_body(*refs):
    *parts, out = refs
    hq = out.shape[1] // 3

    def total(j):
        t = parts[0][:, j * hq : (j + 1) * hq].astype(f32)
        for p in parts[1:]:
            t = t + p[:, j * hq : (j + 1) * hq].astype(f32)
        return t

    a, b, q = total(0), total(1), total(2)
    sigma = jax.nn.sigmoid(a)
    act = a * sigma
    out[:, :hq] = (act * b).astype(bf16)
    out[:, hq : 2 * hq] = (q * b * sigma * (1.0 + a * (1.0 - sigma))).astype(bf16)
    out[:, 2 * hq :] = (q * act).astype(bf16)


def activate(parts, deps):
    vmem = pl.BlockSpec(memory_space=pltpu.VMEM)
    return call(
        activate_body, parts, deps, jax.ShapeDtypeStruct(parts[0].shape, bf16), [vmem] * len(parts), vmem
    )


def backward_body(cap, nb, ndp, dp_ref, *refs):
    pieces, (wg, wu), outs, (dg, du) = refs[:ndp], refs[ndp : ndp + 2], refs[ndp + 2 : -2], refs[-2:]
    hq = pieces[0].shape[1] // 3

    @pl.when(pl.program_id(0) == 0)
    def _():
        for d, piece in enumerate(pieces):
            at = pl.ds(pl.multiple_of((dp_ref[0] ^ d) * hq, hq), hq)
            dg[:, at] = piece[:, hq : 2 * hq]
            du[:, at] = piece[:, 2 * hq :]

    rows = (dot(dg[...], wg[...], 1, 1) + dot(du[...], wu[...], 1, 1)).astype(bf16)
    for i, out in enumerate(outs):
        out[...] = rows[i * cap : (i + 1) * cap]


def backward(cap, nb, ndp, dp_idx, pieces, wg, wu, deps):
    s, h = wg.shape
    return call(
        functools.partial(backward_body, cap, nb, ndp),
        [dp_idx, *pieces, wg, wu],
        deps,
        [jax.ShapeDtypeStruct((cap, s), bf16)] * nb,
        [whole(pieces[0].shape)] * ndp + [pl.BlockSpec((TILE, h), lambda c, i: (c, 0))] * 2,
        [pl.BlockSpec((cap, TILE), lambda c, i: (0, c))] * nb,
        grid=(s // TILE,),
        scalars=1,
        scratch=[pltpu.VMEM((nb * cap, h), bf16)] * 2,
    )


def down_body(cap, sizes, ndp, dp_ref, *refs):
    n_pieces = len(sizes) * ndp
    n_blocks = sum(sizes)
    pieces = refs[:n_pieces]
    blocks = refs[n_pieces : n_pieces + n_blocks]
    wd, mom, new_w, new_m, token, hid_t, dy = refs[n_pieces + n_blocks :]
    hq = pieces[0].shape[1]

    @pl.when(pl.program_id(0) == 0)
    def _():
        token[...] = jnp.zeros_like(token)
        base = 0
        for g, size in enumerate(sizes):
            for d in range(ndp):
                at = pl.ds(pl.multiple_of((dp_ref[0] ^ d) * hq, hq), hq)
                piece = pieces[g * ndp + d][...].astype(f32)
                hid_t[at, base : base + size * cap] = piece.T.astype(bf16)
            base += size * cap

    for i, blk in enumerate(blocks):
        dy[i * cap : (i + 1) * cap, :] = blk[...]
    step_rows = 128
    for c in range(0, hid_t.shape[0], step_rows):
        at = slice(c, c + step_rows)
        grad = dot(hid_t[at, :], dy[...])
        w = wd[at, :].astype(f32)
        blend = first_beta * mom[at, :].astype(f32) + (1.0 - first_beta) * grad
        step = blend * lax.rsqrt(blend * blend + soft_width * soft_width)
        agree = jnp.where((step > 0.0) == (w > 0.0), jnp.abs(step), 0.0)
        new_w[at, :] = (w - learn_rate * (step + decay_rate * agree * w)).astype(bf16)
        new_m[at, :] = blend.astype(bf16)


def down(cap, sizes, ndp, dp_idx, pieces, blocks, wd, mom, deps):
    h, s = wd.shape
    hq = h // ndp
    rows = cap * sum(sizes)
    col = pl.BlockSpec((h, TILE), lambda c, i: (0, c))
    return call(
        functools.partial(down_body, cap, sizes, ndp),
        [dp_idx, *pieces, *blocks, wd, mom],
        deps,
        [jax.ShapeDtypeStruct((h, s), bf16)] * 2 + [jax.ShapeDtypeStruct((8, 128), f32)],
        [whole((p.shape[0], hq)) for p in pieces]
        + [pl.BlockSpec((cap, TILE), lambda c, i: (0, s // TILE + c))] * len(blocks)
        + [col, col],
        [col, col, whole((8, 128))],
        grid=(s // TILE,),
        scalars=1,
        scratch=[pltpu.VMEM((h, rows), bf16), pltpu.VMEM((rows, TILE), bf16)],
    )


def combine_body(cap, offs, chained, me_ref, tgt_ref, *refs):
    nb = len(offs)
    backs = refs[:nb]
    prev = refs[nb] if chained else None
    out, pick_t, rows = refs[-3:]

    @pl.when(pl.program_id(0) == 0)
    def _():
        target = tgt_ref[...]
        slots = lax.broadcasted_iota(jnp.int32, (cap, target.shape[1]), 0)
        hits = [jnp.where(slots + (me_ref[0] ^ k) * cap == target, 1.0, 0.0) for k in offs]
        pick_t[...] = jnp.concatenate(hits, axis=0).T.astype(bf16)

    for i, blk in enumerate(backs):
        rows[i * cap : (i + 1) * cap, :] = blk[...]
    total = dot(pick_t[...], rows[...])
    if chained:
        total = total + prev[...].astype(f32)
    out[...] = total.astype(bf16)


def combine(cap, offs, me, target, backs, prev, deps):
    t = target.shape[1]
    s = backs[0][0].shape[1]
    nb = len(offs)
    wide = s // 2
    col = pl.BlockSpec((t, wide), lambda c, i: (0, c))
    extra = [] if prev is None else [prev]
    return call(
        functools.partial(combine_body, cap, offs, prev is not None),
        [me, target, *[v for v, _ in backs], *extra],
        deps,
        jax.ShapeDtypeStruct((t, s), bf16),
        [whole((1, t))]
        + [pl.BlockSpec((cap, wide), lambda c, i, part=part: (part, c)) for _, part in backs]
        + [col] * len(extra),
        col,
        grid=(s // wide,),
        scalars=1,
        scratch=[pltpu.VMEM((t, nb * cap), bf16), pltpu.VMEM((nb * cap, wide), bf16)],
    )


def local(tokens, grad_out, route_ids, gate_codes, gate_weight, up_weight, down_weight, momentum):
    n = lax.axis_size("expert")
    ndp = lax.axis_size("dp")
    t = tokens.shape[0]
    most = max(2, t * 5 // (4 * n))
    cap = -(-most // 16) * 16
    me = lax.axis_index("expert").astype(jnp.int32).reshape(1)
    dp_idx = lax.axis_index("dp").astype(jnp.int32).reshape(1)
    ids = route_ids.reshape(1, t)
    codes = gate_codes.reshape(1, t)
    wg, wu, wd, mom = gate_weight[0], up_weight[0], down_weight[0], momentum[0]

    def swap_expert(v, k):
        return lax.ppermute(v, "expert", [(i, i ^ k) for i in range(n)])

    def swap_dp(v, k):
        return lax.ppermute(v, "dp", [(i, i ^ k) for i in range(ndp)])

    far, near = grouping(n)
    chunks = [near[0], far[0], far[1] + near[1], far[2] + near[2], far[3]]
    send, got, ready, back, pieces, parts, passed = {}, {}, {}, {}, {}, {}, {}
    mark = []

    def push(offs, deps):
        for k in offs:
            if deps is not None:
                send[k] = after(send[k], mark + deps)
                mark[:] = [send[k]]
            got[k] = swap_expert(send[k], k) if k else send[k]

    def give_back(offs, deps):
        for k in offs:
            rows = ready[k]
            if deps is not None:
                rows = after(rows, mark + deps)
                mark[:] = [rows]
            back[k] = (swap_expert(rows, k) if k else rows, 0)

    def relay(offs, others):
        for k, j in zip(offs, others):
            passed[j] = swap_expert(ready[j], k ^ j)

    def give_both(offs, others, deps):
        for k, j in zip(offs, others):
            rows = join(ready[k], passed[j], mark + deps)
            mark[:] = [rows]
            both = swap_expert(rows, k)
            back[k], back[j] = (both, 0), (both, 1)

    def fwd(c):
        own, *others = forward(cap, ndp, dp_idx, [got[k] for k in chunks[c]], wg, wu, wd, mark)
        mark[:] = [own]
        parts[c] = [own] + [swap_dp(v, d + 1) for d, v in enumerate(others)]

    def act(c):
        own = activate(parts[c], mark)
        mark[:] = [own]
        pieces[c] = [own] + [swap_dp(own, d) for d in range(1, ndp)]

    def bwd(c):
        rows = backward(cap, len(chunks[c]), ndp, dp_idx, pieces[c], wg, wu, mark)
        mark[:] = [rows[0]]
        ready.update(zip(chunks[c], rows))

    def gotten(offs):
        return [got[k] for k in offs]

    offs = far[0] + near[0]
    target, *sends = dispatch(n, cap, offs, me, ids, codes, tokens, grad_out, [])
    send.update(zip(offs, sends))
    mark[:] = [sends[0]]
    push(offs, None)
    offs = far[1] + near[1] + far[2] + near[2] + far[3]
    _, *sends = dispatch(n, cap, offs, me, ids, codes, tokens, grad_out, mark)
    send.update(zip(offs, sends))
    mark[:] = [sends[0]]

    fwd(0)
    push(far[1], [])
    push(near[1], gotten(far[0]))
    act(0)
    fwd(1)
    bwd(0)
    act(1)
    push(far[2], gotten(near[1]))
    push(near[2], gotten(far[1]))
    give_back(near[0], None)
    fwd(2)
    bwd(1)
    act(2)
    push(far[3], gotten(far[2] + near[2]))
    fwd(3)
    bwd(2)
    relay(far[0], far[1])
    act(3)
    give_both(far[0], far[1], gotten(far[3]))
    fwd(4)
    bwd(3)
    give_back(far[2], None)
    act(4)
    bwd(4)
    give_back(far[3], None)
    give_back(near[1], None)
    give_back(near[2], None)
    order = range(len(chunks))
    flat = [k for c in order for k in chunks[c]]
    new_down, new_moment, token = down(
        cap,
        [len(chunks[c]) for c in order],
        ndp,
        dp_idx,
        [p for c in order for p in pieces[c]],
        gotten(flat),
        wd,
        mom,
        mark,
    )
    mark[:] = [token]
    tail = near[1] + near[2] + far[2] + far[3]
    early = [k for k in flat if k not in tail]
    part = combine(cap, early, me, target, [back[k] for k in early], None, mark)
    grad_tokens = combine(cap, tail, me, target, [back[k] for k in tail], part, [])
    return (grad_tokens, new_down[None], new_moment[None])


def solution(mesh):
    placed = (
        P("expert", "dp"),
        P("expert", "dp"),
        P("expert", None),
        P("expert", None),
        P("expert", "dp", None),
        P("expert", "dp", None),
        P("expert", None, "dp"),
        P("expert", None, "dp"),
    )
    return jax.shard_map(
        local,
        mesh=mesh,
        in_specs=placed,
        out_specs=(P("expert", "dp"), P("expert", None, "dp"), P("expert", None, "dp")),
        check_vma=False,
    )
```

```python
import functools

import jax
import jax.numpy as jnp
from jax import lax
from jax.experimental import pallas as pl
from jax.experimental.pallas import tpu as pltpu
from jax.sharding import PartitionSpec as P

first_beta = 0.9
learn_rate = 0.01
decay_rate = 3.0
soft_width = 1.0

TILE = 256
VMEM_BYTES = 24 * 1024 * 1024
LEAD_BYTES = 60 * 1024 * 1024

bf16 = jnp.bfloat16
f32 = jnp.float32


def grouping(n):
    half = n // 2
    step = max(1, half // 4)
    far = [list(range(i, i + step)) for i in range(half, n, step)]
    cuts = [0, half - 2 * step, half - step, half]
    return far, [list(range(i, j)) for i, j in zip(cuts, cuts[1:])]


def skipping(body, n_in, n_deps):
    def run(*refs):
        body(*refs[:n_in], *refs[n_in + n_deps :])

    return run


def call(body, operands, deps, out_shape, in_specs, out_specs, grid=(), scalars=0, scratch=(), aliases=None, limit=VMEM_BYTES):
    any_spec = pl.BlockSpec(memory_space=pl.ANY)
    return pl.pallas_call(
        skipping(body, len(operands), len(deps)),
        out_shape=out_shape,
        grid_spec=pltpu.PrefetchScalarGridSpec(
            num_scalar_prefetch=scalars,
            grid=grid,
            in_specs=list(in_specs) + [any_spec] * len(deps),
            out_specs=out_specs,
            scratch_shapes=list(scratch),
        ),
        input_output_aliases=aliases or {},
        compiler_params=pltpu.CompilerParams(vmem_limit_bytes=limit),
        cost_estimate=pl.CostEstimate(flops=0, bytes_accessed=0, transcendentals=0),
    )(*operands, *deps)


def dot(a, b, ca=1, cb=0):
    return lax.dot_general(a, b, (((ca,), (cb,)), ((), ())), preferred_element_type=f32)


def whole(shape):
    return pl.BlockSpec(shape, lambda *_: (0,) * len(shape))


def after_body(*refs):
    pass


def after(value, deps):
    any_spec = pl.BlockSpec(memory_space=pl.ANY)
    return call(
        after_body, [value], deps, jax.ShapeDtypeStruct(value.shape, value.dtype), [any_spec], any_spec, aliases={0: 0}
    )


def picks(cap, offs, me, target, scale):
    slots = lax.broadcasted_iota(jnp.int32, (cap, target.shape[1]), 0)
    hits = [slots + (me ^ k) * cap == target for k in offs]
    pick = jnp.concatenate([jnp.where(h, 1.0, 0.0).astype(bf16) for h in hits], axis=0)
    scaled = jnp.concatenate([jnp.where(h, scale, 0.0).astype(bf16) for h in hits], axis=0)
    return pick, scaled


def dispatch_body(n, cap, offs, cuts, me_ref, ids_ref, codes_ref, x_ref, g_ref, target_ref, *refs):
    *outs, ids_v, codes_v, x_v, g_v, sems = refs
    small = [
        pltpu.make_async_copy(ids_ref, ids_v, sems.at[0]),
        pltpu.make_async_copy(codes_ref, codes_v, sems.at[1]),
    ]
    large = [[], []]
    for which, (ref, buf) in enumerate(((x_ref, x_v), (g_ref, g_v))):
        for r0, r1 in cuts:
            at = sems.at[2 + which * len(cuts) + len(large[which])]
            large[which].append(pltpu.make_async_copy(ref.at[r0:r1, :], buf.at[r0:r1, :], at))
    for copy in small + large[0] + large[1]:
        copy.start()
    small[0].wait()
    ids = ids_v[...]
    t, s = x_v.shape
    hot = (lax.broadcasted_iota(jnp.int32, (n, t), 0) == ids).astype(f32)
    before = (
        lax.broadcasted_iota(jnp.int32, (t, t), 0) < lax.broadcasted_iota(jnp.int32, (t, t), 1)
    ).astype(f32)
    counts = dot(hot.astype(bf16), before.astype(bf16))
    rank = jnp.sum(hot * counts, axis=0, keepdims=True).astype(jnp.int32)
    target = ids * cap + rank
    target_ref[...] = target
    small[1].wait()
    pick, scaled = picks(cap, offs, me_ref[0], target, codes_v[...].astype(f32) / 256.0)
    for left, buf, base, copies in ((pick, x_v, 0, large[0]), (scaled, g_v, s, large[1])):
        for copy in copies:
            copy.wait()
        for c in range(0, s, TILE):
            rows = dot(left, buf[:, c : c + TILE]).astype(bf16)
            for i, out in enumerate(outs):
                out[:, base + c : base + c + TILE] = rows[i * cap : (i + 1) * cap]


def dispatch(n, cap, offs, me, ids, codes, x, g, deps):
    t, s = x.shape
    cuts = [(r, r + t // 4) for r in range(0, t, t // 4)]
    out_shape = [jax.ShapeDtypeStruct((1, t), jnp.int32)] + [jax.ShapeDtypeStruct((cap, 2 * s), bf16) for _ in offs]
    far_memory = pl.BlockSpec(memory_space=pltpu.HBM)
    return call(
        functools.partial(dispatch_body, n, cap, offs, cuts),
        [me, ids, codes, x, g],
        deps,
        out_shape,
        [pl.BlockSpec(memory_space=pltpu.SMEM)] + [far_memory] * 4,
        [pl.BlockSpec(memory_space=pltpu.VMEM)] * len(out_shape),
        scratch=[
            pltpu.VMEM((1, t), jnp.int32),
            pltpu.VMEM((1, t), jnp.int32),
            pltpu.VMEM((t, s), bf16),
            pltpu.VMEM((t, s), bf16),
            pltpu.SemaphoreType.DMA((2 + 2 * len(cuts),)),
        ],
        limit=LEAD_BYTES,
    )


def join_body(first, second, out):
    cap = first.shape[0]
    out[:cap, :] = first[...]
    out[cap:, :] = second[...]


def join(first, second, deps):
    cap, s = first.shape
    vmem = pl.BlockSpec(memory_space=pltpu.VMEM)
    return call(join_body, [first, second], deps, jax.ShapeDtypeStruct((2 * cap, s), bf16), [vmem] * 2, vmem)


def forward_body(cap, nb, ndp, dp_ref, *refs):
    blocks, (wg, wu, wd), outs, rows = refs[:nb], refs[nb : nb + 3], refs[nb + 3 : -1], refs[-1]
    d = pl.program_id(0)
    s = wg.shape[0]
    hq = wg.shape[1]

    @pl.when(d == 0)
    def _():
        for i, blk in enumerate(blocks):
            rows[i * cap : (i + 1) * cap, :] = blk[...]

    x = rows[:, :s]
    r = rows[:, s:]
    a = dot(x, wg[...]).astype(bf16)
    b = dot(x, wu[...]).astype(bf16)
    q = dot(r, wd[...], 1, 1).astype(bf16)
    for k in range(ndp):

        @pl.when(d == k)
        def _():
            outs[k][:, :hq] = a
            outs[k][:, hq : 2 * hq] = b
            outs[k][:, 2 * hq :] = q


def forward(cap, ndp, dp_idx, blocks, wg, wu, wd, deps):
    s, h = wg.shape
    hq = h // ndp
    nb = len(blocks)
    rows = nb * cap
    return call(
        functools.partial(forward_body, cap, nb, ndp),
        [dp_idx, *blocks, wg, wu, wd],
        deps,
        [jax.ShapeDtypeStruct((rows, 3 * hq), bf16)] * ndp,
        [whole((cap, 2 * s))] * nb
        + [pl.BlockSpec((s, hq), lambda d, i: (0, i[0] ^ d))] * 2
        + [pl.BlockSpec((hq, s), lambda d, i: (i[0] ^ d, 0))],
        [whole((rows, 3 * hq))] * ndp,
        grid=(ndp,),
        scalars=1,
        scratch=[pltpu.VMEM((rows, 2 * s), bf16)],
    )


def activate_body(*refs):
    *parts, out = refs
    hq = out.shape[1] // 3

    def total(j):
        t = parts[0][:, j * hq : (j + 1) * hq].astype(f32)
        for p in parts[1:]:
            t = t + p[:, j * hq : (j + 1) * hq].astype(f32)
        return t

    a, b, q = total(0), total(1), total(2)
    sigma = jax.nn.sigmoid(a)
    act = a * sigma
    out[:, :hq] = (act * b).astype(bf16)
    out[:, hq : 2 * hq] = (q * b * sigma * (1.0 + a * (1.0 - sigma))).astype(bf16)
    out[:, 2 * hq :] = (q * act).astype(bf16)


def activate(parts, deps):
    vmem = pl.BlockSpec(memory_space=pltpu.VMEM)
    return call(
        activate_body, parts, deps, jax.ShapeDtypeStruct(parts[0].shape, bf16), [vmem] * len(parts), vmem
    )


def backward_body(cap, nb, ndp, dp_ref, *refs):
    pieces, (wg, wu), outs, (dg, du) = refs[:ndp], refs[ndp : ndp + 2], refs[ndp + 2 : -2], refs[-2:]
    hq = pieces[0].shape[1] // 3

    @pl.when(pl.program_id(0) == 0)
    def _():
        for d, piece in enumerate(pieces):
            at = pl.ds(pl.multiple_of((dp_ref[0] ^ d) * hq, hq), hq)
            dg[:, at] = piece[:, hq : 2 * hq]
            du[:, at] = piece[:, 2 * hq :]

    rows = (dot(dg[...], wg[...], 1, 1) + dot(du[...], wu[...], 1, 1)).astype(bf16)
    for i, out in enumerate(outs):
        out[...] = rows[i * cap : (i + 1) * cap]


def backward(cap, nb, ndp, dp_idx, pieces, wg, wu, deps):
    s, h = wg.shape
    return call(
        functools.partial(backward_body, cap, nb, ndp),
        [dp_idx, *pieces, wg, wu],
        deps,
        [jax.ShapeDtypeStruct((cap, s), bf16)] * nb,
        [whole(pieces[0].shape)] * ndp + [pl.BlockSpec((TILE, h), lambda c, i: (c, 0))] * 2,
        [pl.BlockSpec((cap, TILE), lambda c, i: (0, c))] * nb,
        grid=(s // TILE,),
        scalars=1,
        scratch=[pltpu.VMEM((nb * cap, h), bf16)] * 2,
    )


def down_body(cap, sizes, ndp, dp_ref, *refs):
    n_pieces = len(sizes) * ndp
    n_blocks = sum(sizes)
    pieces = refs[:n_pieces]
    blocks = refs[n_pieces : n_pieces + n_blocks]
    wd, mom, new_w, new_m, token, hid_t, dy = refs[n_pieces + n_blocks :]
    hq = pieces[0].shape[1]

    @pl.when(pl.program_id(0) == 0)
    def _():
        token[...] = jnp.zeros_like(token)
        base = 0
        for g, size in enumerate(sizes):
            for d in range(ndp):
                at = pl.ds(pl.multiple_of((dp_ref[0] ^ d) * hq, hq), hq)
                piece = pieces[g * ndp + d][...].astype(f32)
                hid_t[at, base : base + size * cap] = piece.T.astype(bf16)
            base += size * cap

    for i, blk in enumerate(blocks):
        dy[i * cap : (i + 1) * cap, :] = blk[...]
    step_rows = 128
    for c in range(0, hid_t.shape[0], step_rows):
        at = slice(c, c + step_rows)
        grad = dot(hid_t[at, :], dy[...])
        w = wd[at, :].astype(f32)
        blend = first_beta * mom[at, :].astype(f32) + (1.0 - first_beta) * grad
        step = blend * lax.rsqrt(blend * blend + soft_width * soft_width)
        agree = jnp.where((step > 0.0) == (w > 0.0), jnp.abs(step), 0.0)
        new_w[at, :] = (w - learn_rate * (step + decay_rate * agree * w)).astype(bf16)
        new_m[at, :] = blend.astype(bf16)


def down(cap, sizes, ndp, dp_idx, pieces, blocks, wd, mom, deps):
    h, s = wd.shape
    hq = h // ndp
    rows = cap * sum(sizes)
    col = pl.BlockSpec((h, TILE), lambda c, i: (0, c))
    return call(
        functools.partial(down_body, cap, sizes, ndp),
        [dp_idx, *pieces, *blocks, wd, mom],
        deps,
        [jax.ShapeDtypeStruct((h, s), bf16)] * 2 + [jax.ShapeDtypeStruct((8, 128), f32)],
        [whole((p.shape[0], hq)) for p in pieces]
        + [pl.BlockSpec((cap, TILE), lambda c, i: (0, s // TILE + c))] * len(blocks)
        + [col, col],
        [col, col, whole((8, 128))],
        grid=(s // TILE,),
        scalars=1,
        scratch=[pltpu.VMEM((h, rows), bf16), pltpu.VMEM((rows, TILE), bf16)],
    )


def combine_body(cap, offs, chained, me_ref, tgt_ref, *refs):
    nb = len(offs)
    backs = refs[:nb]
    prev = refs[nb] if chained else None
    out, pick_t, rows = refs[-3:]
    part = out.shape[0]
    i = pl.program_id(0)

    @pl.when(i == 0)
    def _():
        target = tgt_ref[...]
        slots = lax.broadcasted_iota(jnp.int32, (cap, target.shape[1]), 0)
        hits = [jnp.where(slots + (me_ref[0] ^ k) * cap == target, 1.0, 0.0) for k in offs]
        pick_t[...] = jnp.concatenate(hits, axis=0).T.astype(bf16)
        for j, blk in enumerate(backs):
            rows[j * cap : (j + 1) * cap, :] = blk[...]

    total = dot(pick_t[pl.ds(pl.multiple_of(i * part, part), part), :], rows[...])
    if chained:
        total = total + prev[...].astype(f32)
    out[...] = total.astype(bf16)


def combine(cap, offs, me, target, backs, prev, deps):
    t = target.shape[1]
    s = backs[0][0].shape[1]
    nb = len(offs)
    part = t // 2
    block = pl.BlockSpec((part, s), lambda c, i: (c, 0))
    extra = [] if prev is None else [prev]
    return call(
        functools.partial(combine_body, cap, offs, prev is not None),
        [me, target, *[v for v, _ in backs], *extra],
        deps,
        jax.ShapeDtypeStruct((t, s), bf16),
        [whole((1, t))]
        + [pl.BlockSpec((cap, s), lambda c, i, at=at: (at, 0)) for _, at in backs]
        + [block] * len(extra),
        block,
        grid=(2,),
        scalars=1,
        scratch=[pltpu.VMEM((t, nb * cap), bf16), pltpu.VMEM((nb * cap, s), bf16)],
    )


def local(tokens, grad_out, route_ids, gate_codes, gate_weight, up_weight, down_weight, momentum):
    n = lax.axis_size("expert")
    ndp = lax.axis_size("dp")
    t = tokens.shape[0]
    most = max(2, t * 5 // (4 * n))
    cap = -(-most // 16) * 16
    me = lax.axis_index("expert").astype(jnp.int32).reshape(1)
    dp_idx = lax.axis_index("dp").astype(jnp.int32).reshape(1)
    ids = route_ids.reshape(1, t)
    codes = gate_codes.reshape(1, t)
    wg, wu, wd, mom = gate_weight[0], up_weight[0], down_weight[0], momentum[0]

    def swap_expert(v, k):
        return lax.ppermute(v, "expert", [(i, i ^ k) for i in range(n)])

    def swap_dp(v, k):
        return lax.ppermute(v, "dp", [(i, i ^ k) for i in range(ndp)])

    far, near = grouping(n)
    chunks = [near[0], far[0], far[1] + near[1], far[2] + near[2], far[3]]
    send, got, ready, back, pieces, parts, passed = {}, {}, {}, {}, {}, {}, {}
    mark = []

    def push(offs, deps):
        for k in offs:
            if deps is not None:
                send[k] = after(send[k], mark + deps)
                mark[:] = [send[k]]
            got[k] = swap_expert(send[k], k) if k else send[k]

    def give_back(offs, deps):
        for k in offs:
            rows = ready[k]
            if deps is not None:
                rows = after(rows, mark + deps)
                mark[:] = [rows]
            back[k] = (swap_expert(rows, k) if k else rows, 0)

    def relay(offs, others):
        for k, j in zip(offs, others):
            passed[j] = swap_expert(ready[j], k ^ j)

    def give_both(offs, others, deps):
        for k, j in zip(offs, others):
            rows = join(ready[k], passed[j], mark + deps)
            mark[:] = [rows]
            both = swap_expert(rows, k)
            back[k], back[j] = (both, 0), (both, 1)

    def fwd(c):
        own, *others = forward(cap, ndp, dp_idx, [got[k] for k in chunks[c]], wg, wu, wd, mark)
        mark[:] = [own]
        parts[c] = [own] + [swap_dp(v, d + 1) for d, v in enumerate(others)]

    def act(c):
        own = activate(parts[c], mark)
        mark[:] = [own]
        pieces[c] = [own] + [swap_dp(own, d) for d in range(1, ndp)]

    def bwd(c):
        rows = backward(cap, len(chunks[c]), ndp, dp_idx, pieces[c], wg, wu, mark)
        mark[:] = [rows[0]]
        ready.update(zip(chunks[c], rows))

    def gotten(offs):
        return [got[k] for k in offs]

    own, swapped = near[0][:1], near[0][1:]
    offs = far[0] + swapped
    target, *sends = dispatch(n, cap, offs, me, ids, codes, tokens, grad_out, [])
    send.update(zip(offs, sends))
    mark[:] = [sends[0]]
    push(offs, None)
    offs = own + far[1] + near[1] + far[2] + near[2] + far[3]
    _, *sends = dispatch(n, cap, offs, me, ids, codes, tokens, grad_out, mark)
    send.update(zip(offs, sends))
    mark[:] = [sends[0]]
    push(own, None)

    fwd(0)
    push(far[1], [])
    push(near[1], gotten(far[0]))
    act(0)
    fwd(1)
    bwd(0)
    act(1)
    push(far[2], gotten(near[1]))
    push(near[2], gotten(far[1]))
    give_back(near[0], None)
    fwd(2)
    bwd(1)
    act(2)
    push(far[3], gotten(far[2] + near[2]))
    fwd(3)
    bwd(2)
    relay(far[0], far[1])
    act(3)
    give_both(far[0], far[1], gotten(far[3]))
    fwd(4)
    bwd(3)
    give_back(far[2], None)
    act(4)
    bwd(4)
    give_back(far[3], None)
    give_back(near[1], None)
    order = range(len(chunks))
    flat = [k for c in order for k in chunks[c]]
    new_down, new_moment, token = down(
        cap,
        [len(chunks[c]) for c in order],
        ndp,
        dp_idx,
        [p for c in order for p in pieces[c]],
        gotten(flat),
        wd,
        mom,
        mark,
    )
    mark[:] = [token]
    give_back(near[2], None)
    tail = far[1] + near[2] + far[3]
    early = [k for k in flat if k not in tail]
    part = combine(cap, early, me, target, [back[k] for k in early], None, mark)
    grad_tokens = combine(cap, tail, me, target, [back[k] for k in tail], part, [])
    return (grad_tokens, new_down[None], new_moment[None])


def solution(mesh):
    placed = (
        P("expert", "dp"),
        P("expert", "dp"),
        P("expert", None),
        P("expert", None),
        P("expert", "dp", None),
        P("expert", "dp", None),
        P("expert", None, "dp"),
        P("expert", None, "dp"),
    )
    return jax.shard_map(
        local,
        mesh=mesh,
        in_specs=placed,
        out_specs=(P("expert", "dp"), P("expert", None, "dp"), P("expert", None, "dp")),
        check_vma=False,
    )
```

```python
import functools

import jax
import jax.numpy as jnp
from jax import lax
from jax.experimental import pallas as pl
from jax.experimental.pallas import tpu as pltpu
from jax.sharding import PartitionSpec as P

first_beta = 0.9
learn_rate = 0.01
decay_rate = 3.0
soft_width = 1.0

TILE = 256
VMEM_BYTES = 24 * 1024 * 1024
LEAD_BYTES = 60 * 1024 * 1024

bf16 = jnp.bfloat16
f32 = jnp.float32


def grouping(n):
    half = n // 2
    step = max(1, half // 4)
    far = [list(range(i, i + step)) for i in range(half, n, step)]
    cuts = [0, half - 2 * step, half - step, half]
    return far, [list(range(i, j)) for i, j in zip(cuts, cuts[1:])]


def skipping(body, n_in, n_deps):
    def run(*refs):
        body(*refs[:n_in], *refs[n_in + n_deps :])

    return run


def call(body, operands, deps, out_shape, in_specs, out_specs, grid=(), scalars=0, scratch=(), aliases=None, limit=VMEM_BYTES):
    any_spec = pl.BlockSpec(memory_space=pl.ANY)
    return pl.pallas_call(
        skipping(body, len(operands), len(deps)),
        out_shape=out_shape,
        grid_spec=pltpu.PrefetchScalarGridSpec(
            num_scalar_prefetch=scalars,
            grid=grid,
            in_specs=list(in_specs) + [any_spec] * len(deps),
            out_specs=out_specs,
            scratch_shapes=list(scratch),
        ),
        input_output_aliases=aliases or {},
        compiler_params=pltpu.CompilerParams(vmem_limit_bytes=limit),
        cost_estimate=pl.CostEstimate(flops=0, bytes_accessed=0, transcendentals=0),
    )(*operands, *deps)


def dot(a, b, ca=1, cb=0):
    return lax.dot_general(a, b, (((ca,), (cb,)), ((), ())), preferred_element_type=f32)


def whole(shape):
    return pl.BlockSpec(shape, lambda *_: (0,) * len(shape))


def after_body(*refs):
    pass


def after(value, deps):
    any_spec = pl.BlockSpec(memory_space=pl.ANY)
    return call(
        after_body, [value], deps, jax.ShapeDtypeStruct(value.shape, value.dtype), [any_spec], any_spec, aliases={0: 0}
    )


def picks(cap, offs, me, target, scale):
    slots = lax.broadcasted_iota(jnp.int32, (cap, target.shape[1]), 0)
    hits = [slots + (me ^ k) * cap == target for k in offs]
    pick = jnp.concatenate([jnp.where(h, 1.0, 0.0).astype(bf16) for h in hits], axis=0)
    scaled = jnp.concatenate([jnp.where(h, scale, 0.0).astype(bf16) for h in hits], axis=0)
    return pick, scaled


def dispatch_body(n, cap, offs, cuts, me_ref, ids_ref, codes_ref, x_ref, g_ref, target_ref, *refs):
    *outs, ids_v, codes_v, x_v, g_v, sems = refs
    small = [
        pltpu.make_async_copy(ids_ref, ids_v, sems.at[0]),
        pltpu.make_async_copy(codes_ref, codes_v, sems.at[1]),
    ]
    large = [[], []]
    for which, (ref, buf) in enumerate(((x_ref, x_v), (g_ref, g_v))):
        for r0, r1 in cuts:
            at = sems.at[2 + which * len(cuts) + len(large[which])]
            large[which].append(pltpu.make_async_copy(ref.at[r0:r1, :], buf.at[r0:r1, :], at))
    for copy in small + large[0] + large[1]:
        copy.start()
    small[0].wait()
    ids = ids_v[...]
    t, s = x_v.shape
    hot = (lax.broadcasted_iota(jnp.int32, (n, t), 0) == ids).astype(f32)
    before = (
        lax.broadcasted_iota(jnp.int32, (t, t), 0) < lax.broadcasted_iota(jnp.int32, (t, t), 1)
    ).astype(f32)
    counts = dot(hot.astype(bf16), before.astype(bf16))
    rank = jnp.sum(hot * counts, axis=0, keepdims=True).astype(jnp.int32)
    target = ids * cap + rank
    target_ref[...] = target
    small[1].wait()
    pick, scaled = picks(cap, offs, me_ref[0], target, codes_v[...].astype(f32) / 256.0)
    for left, buf, base, copies in ((pick, x_v, 0, large[0]), (scaled, g_v, s, large[1])):
        for copy in copies:
            copy.wait()
        for c in range(0, s, TILE):
            rows = dot(left, buf[:, c : c + TILE]).astype(bf16)
            for i, out in enumerate(outs):
                out[:, base + c : base + c + TILE] = rows[i * cap : (i + 1) * cap]


def dispatch(n, cap, offs, me, ids, codes, x, g, deps):
    t, s = x.shape
    cuts = [(r, r + t // 4) for r in range(0, t, t // 4)]
    out_shape = [jax.ShapeDtypeStruct((1, t), jnp.int32)] + [jax.ShapeDtypeStruct((cap, 2 * s), bf16) for _ in offs]
    far_memory = pl.BlockSpec(memory_space=pltpu.HBM)
    return call(
        functools.partial(dispatch_body, n, cap, offs, cuts),
        [me, ids, codes, x, g],
        deps,
        out_shape,
        [pl.BlockSpec(memory_space=pltpu.SMEM)] + [far_memory] * 4,
        [pl.BlockSpec(memory_space=pltpu.VMEM)] * len(out_shape),
        scratch=[
            pltpu.VMEM((1, t), jnp.int32),
            pltpu.VMEM((1, t), jnp.int32),
            pltpu.VMEM((t, s), bf16),
            pltpu.VMEM((t, s), bf16),
            pltpu.SemaphoreType.DMA((2 + 2 * len(cuts),)),
        ],
        limit=LEAD_BYTES,
    )


def join_body(first, second, out):
    cap = first.shape[0]
    out[:cap, :] = first[...]
    out[cap:, :] = second[...]


def join(first, second, deps):
    cap, s = first.shape
    vmem = pl.BlockSpec(memory_space=pltpu.VMEM)
    return call(join_body, [first, second], deps, jax.ShapeDtypeStruct((2 * cap, s), bf16), [vmem] * 2, vmem)


def forward_body(cap, nb, ndp, dp_ref, *refs):
    blocks, (wg, wu, wd), outs, rows = refs[:nb], refs[nb : nb + 3], refs[nb + 3 : -1], refs[-1]
    d = pl.program_id(0)
    s = wg.shape[0]
    hq = wg.shape[1]

    @pl.when(d == 0)
    def _():
        for i, blk in enumerate(blocks):
            rows[i * cap : (i + 1) * cap, :] = blk[...]

    x = rows[:, :s]
    r = rows[:, s:]
    a = dot(x, wg[...]).astype(bf16)
    b = dot(x, wu[...]).astype(bf16)
    q = dot(r, wd[...], 1, 1).astype(bf16)
    for k in range(ndp):

        @pl.when(d == k)
        def _():
            outs[k][:, :hq] = a
            outs[k][:, hq : 2 * hq] = b
            outs[k][:, 2 * hq :] = q


def forward(cap, ndp, dp_idx, blocks, wg, wu, wd, deps):
    s, h = wg.shape
    hq = h // ndp
    nb = len(blocks)
    rows = nb * cap
    return call(
        functools.partial(forward_body, cap, nb, ndp),
        [dp_idx, *blocks, wg, wu, wd],
        deps,
        [jax.ShapeDtypeStruct((rows, 3 * hq), bf16)] * ndp,
        [whole((cap, 2 * s))] * nb
        + [pl.BlockSpec((s, hq), lambda d, i: (0, i[0] ^ d))] * 2
        + [pl.BlockSpec((hq, s), lambda d, i: (i[0] ^ d, 0))],
        [whole((rows, 3 * hq))] * ndp,
        grid=(ndp,),
        scalars=1,
        scratch=[pltpu.VMEM((rows, 2 * s), bf16)],
    )


def activate_body(*refs):
    *parts, out = refs
    hq = out.shape[1] // 3

    def total(j):
        t = parts[0][:, j * hq : (j + 1) * hq].astype(f32)
        for p in parts[1:]:
            t = t + p[:, j * hq : (j + 1) * hq].astype(f32)
        return t

    a, b, q = total(0), total(1), total(2)
    sigma = jax.nn.sigmoid(a)
    act = a * sigma
    out[:, :hq] = (act * b).astype(bf16)
    out[:, hq : 2 * hq] = (q * b * sigma * (1.0 + a * (1.0 - sigma))).astype(bf16)
    out[:, 2 * hq :] = (q * act).astype(bf16)


def activate(parts, deps):
    vmem = pl.BlockSpec(memory_space=pltpu.VMEM)
    return call(
        activate_body, parts, deps, jax.ShapeDtypeStruct(parts[0].shape, bf16), [vmem] * len(parts), vmem
    )


def backward_body(cap, nb, ndp, dp_ref, *refs):
    pieces, (wg, wu), outs, (dg, du) = refs[:ndp], refs[ndp : ndp + 2], refs[ndp + 2 : -2], refs[-2:]
    hq = pieces[0].shape[1] // 3

    @pl.when(pl.program_id(0) == 0)
    def _():
        for d, piece in enumerate(pieces):
            at = pl.ds(pl.multiple_of((dp_ref[0] ^ d) * hq, hq), hq)
            dg[:, at] = piece[:, hq : 2 * hq]
            du[:, at] = piece[:, 2 * hq :]

    rows = (dot(dg[...], wg[...], 1, 1) + dot(du[...], wu[...], 1, 1)).astype(bf16)
    for i, out in enumerate(outs):
        out[...] = rows[i * cap : (i + 1) * cap]


def backward(cap, nb, ndp, dp_idx, pieces, wg, wu, deps):
    s, h = wg.shape
    return call(
        functools.partial(backward_body, cap, nb, ndp),
        [dp_idx, *pieces, wg, wu],
        deps,
        [jax.ShapeDtypeStruct((cap, s), bf16)] * nb,
        [whole(pieces[0].shape)] * ndp + [pl.BlockSpec((TILE, h), lambda c, i: (c, 0))] * 2,
        [pl.BlockSpec((cap, TILE), lambda c, i: (0, c))] * nb,
        grid=(s // TILE,),
        scalars=1,
        scratch=[pltpu.VMEM((nb * cap, h), bf16)] * 2,
    )


def down_body(cap, sizes, ndp, dp_ref, *refs):
    n_pieces = len(sizes) * ndp
    n_blocks = sum(sizes)
    pieces = refs[:n_pieces]
    blocks = refs[n_pieces : n_pieces + n_blocks]
    wd, mom, new_w, new_m, token, hid_t, dy = refs[n_pieces + n_blocks :]
    hq = pieces[0].shape[1]

    @pl.when(pl.program_id(0) == 0)
    def _():
        token[...] = jnp.zeros_like(token)
        base = 0
        for g, size in enumerate(sizes):
            for d in range(ndp):
                at = pl.ds(pl.multiple_of((dp_ref[0] ^ d) * hq, hq), hq)
                piece = pieces[g * ndp + d][...].astype(f32)
                hid_t[at, base : base + size * cap] = piece.T.astype(bf16)
            base += size * cap

    for i, blk in enumerate(blocks):
        dy[i * cap : (i + 1) * cap, :] = blk[...]
    step_rows = 128
    for c in range(0, hid_t.shape[0], step_rows):
        at = slice(c, c + step_rows)
        grad = dot(hid_t[at, :], dy[...])
        w = wd[at, :].astype(f32)
        blend = first_beta * mom[at, :].astype(f32) + (1.0 - first_beta) * grad
        step = blend * lax.rsqrt(blend * blend + soft_width * soft_width)
        agree = jnp.where((step > 0.0) == (w > 0.0), jnp.abs(step), 0.0)
        new_w[at, :] = (w - learn_rate * (step + decay_rate * agree * w)).astype(bf16)
        new_m[at, :] = blend.astype(bf16)


def down(cap, sizes, ndp, dp_idx, pieces, blocks, wd, mom, deps):
    h, s = wd.shape
    hq = h // ndp
    rows = cap * sum(sizes)
    col = pl.BlockSpec((h, TILE), lambda c, i: (0, c))
    return call(
        functools.partial(down_body, cap, sizes, ndp),
        [dp_idx, *pieces, *blocks, wd, mom],
        deps,
        [jax.ShapeDtypeStruct((h, s), bf16)] * 2 + [jax.ShapeDtypeStruct((8, 128), f32)],
        [whole((p.shape[0], hq)) for p in pieces]
        + [pl.BlockSpec((cap, TILE), lambda c, i: (0, s // TILE + c))] * len(blocks)
        + [col, col],
        [col, col, whole((8, 128))],
        grid=(s // TILE,),
        scalars=1,
        scratch=[pltpu.VMEM((h, rows), bf16), pltpu.VMEM((rows, TILE), bf16)],
    )


def transposed_picks(cap, offs, me, target):
    slots = lax.broadcasted_iota(jnp.int32, (cap, target.shape[1]), 0)
    hits = [jnp.where(slots + (me ^ k) * cap == target, 1.0, 0.0) for k in offs]
    return jnp.concatenate(hits, axis=0).T.astype(bf16)


def combine_body(cap, offs, later, me_ref, tgt_ref, *refs):
    nb = len(offs)
    backs, (out, later_picks, picks, rows) = refs[:nb], refs[nb:]
    part = out.shape[0]
    i = pl.program_id(0)

    @pl.when(i == 0)
    def _():
        picks[...] = transposed_picks(cap, offs, me_ref[0], tgt_ref[...])
        later_picks[...] = transposed_picks(cap, later, me_ref[0], tgt_ref[...])
        for j, blk in enumerate(backs):
            rows[j * cap : (j + 1) * cap, :] = blk[...]

    out[...] = dot(picks[pl.ds(pl.multiple_of(i * part, part), part), :], rows[...]).astype(bf16)


def combine(cap, offs, later, me, target, backs, deps):
    t = target.shape[1]
    s = backs[0][0].shape[1]
    nb = len(offs)
    part = t // 2
    return call(
        functools.partial(combine_body, cap, offs, later),
        [me, target, *[v for v, _ in backs]],
        deps,
        [jax.ShapeDtypeStruct((t, s), bf16), jax.ShapeDtypeStruct((t, len(later) * cap), bf16)],
        [whole((1, t))] + [pl.BlockSpec((cap, s), lambda c, i, at=at: (at, 0)) for _, at in backs],
        [pl.BlockSpec((part, s), lambda c, i: (c, 0)), whole((t, len(later) * cap))],
        grid=(2,),
        scalars=1,
        scratch=[pltpu.VMEM((t, nb * cap), bf16), pltpu.VMEM((nb * cap, s), bf16)],
    )


def finish_body(cap, nb, picks, prev, *refs):
    backs, (out, rows) = refs[:nb], refs[nb:]

    @pl.when(pl.program_id(0) == 0)
    def _():
        for j, blk in enumerate(backs):
            rows[j * cap : (j + 1) * cap, :] = blk[...]

    out[...] = (dot(picks[...], rows[...]) + prev[...].astype(f32)).astype(bf16)


def finish(cap, picks, prev, backs):
    t, s = prev.shape
    nb = len(backs)
    part = t // 2
    block = pl.BlockSpec((part, s), lambda c: (c, 0))
    return call(
        functools.partial(finish_body, cap, nb),
        [picks, prev, *[v for v, _ in backs]],
        [],
        jax.ShapeDtypeStruct((t, s), bf16),
        [pl.BlockSpec((part, nb * cap), lambda c: (c, 0)), block]
        + [pl.BlockSpec((cap, s), lambda c, at=at: (at, 0)) for _, at in backs],
        block,
        grid=(2,),
        scratch=[pltpu.VMEM((nb * cap, s), bf16)],
    )


def local(tokens, grad_out, route_ids, gate_codes, gate_weight, up_weight, down_weight, momentum):
    n = lax.axis_size("expert")
    ndp = lax.axis_size("dp")
    t = tokens.shape[0]
    most = max(2, t * 5 // (4 * n))
    cap = -(-most // 16) * 16
    me = lax.axis_index("expert").astype(jnp.int32).reshape(1)
    dp_idx = lax.axis_index("dp").astype(jnp.int32).reshape(1)
    ids = route_ids.reshape(1, t)
    codes = gate_codes.reshape(1, t)
    wg, wu, wd, mom = gate_weight[0], up_weight[0], down_weight[0], momentum[0]

    def swap_expert(v, k):
        return lax.ppermute(v, "expert", [(i, i ^ k) for i in range(n)])

    def swap_dp(v, k):
        return lax.ppermute(v, "dp", [(i, i ^ k) for i in range(ndp)])

    far, near = grouping(n)
    chunks = [near[0], far[0], far[1] + near[1], far[2] + near[2], far[3]]
    send, got, ready, back, pieces, parts, passed = {}, {}, {}, {}, {}, {}, {}
    mark = []

    def push(offs, deps):
        for k in offs:
            if deps is not None:
                send[k] = after(send[k], mark + deps)
                mark[:] = [send[k]]
            got[k] = swap_expert(send[k], k) if k else send[k]

    def give_back(offs, deps):
        for k in offs:
            rows = ready[k]
            if deps is not None:
                rows = after(rows, mark + deps)
                mark[:] = [rows]
            back[k] = (swap_expert(rows, k) if k else rows, 0)

    def relay(offs, others):
        for k, j in zip(offs, others):
            passed[j] = swap_expert(ready[j], k ^ j)

    def give_both(offs, others, deps):
        for k, j in zip(offs, others):
            rows = join(ready[k], passed[j], mark + deps)
            mark[:] = [rows]
            both = swap_expert(rows, k)
            back[k], back[j] = (both, 0), (both, 1)

    def fwd(c):
        own, *others = forward(cap, ndp, dp_idx, [got[k] for k in chunks[c]], wg, wu, wd, mark)
        mark[:] = [own]
        parts[c] = [own] + [swap_dp(v, d + 1) for d, v in enumerate(others)]

    def act(c):
        own = activate(parts[c], mark)
        mark[:] = [own]
        pieces[c] = [own] + [swap_dp(own, d) for d in range(1, ndp)]

    def bwd(c):
        rows = backward(cap, len(chunks[c]), ndp, dp_idx, pieces[c], wg, wu, mark)
        mark[:] = [rows[0]]
        ready.update(zip(chunks[c], rows))

    def gotten(offs):
        return [got[k] for k in offs]

    own, swapped = near[0][:1], near[0][1:]
    offs = far[0] + swapped
    target, *sends = dispatch(n, cap, offs, me, ids, codes, tokens, grad_out, [])
    send.update(zip(offs, sends))
    mark[:] = [sends[0]]
    push(offs, None)
    offs = own + far[1] + near[1] + far[2] + near[2] + far[3]
    _, *sends = dispatch(n, cap, offs, me, ids, codes, tokens, grad_out, mark)
    send.update(zip(offs, sends))
    mark[:] = [sends[0]]
    push(own, None)

    fwd(0)
    push(far[1], [])
    push(near[1], gotten(far[0]))
    act(0)
    fwd(1)
    bwd(0)
    act(1)
    push(far[2], gotten(near[1]))
    push(near[2], gotten(far[1]))
    give_back(near[0], None)
    fwd(2)
    bwd(1)
    act(2)
    push(far[3], gotten(far[2] + near[2]))
    fwd(3)
    bwd(2)
    relay(far[0], far[1])
    act(3)
    give_both(far[0], far[1], gotten(far[3]))
    fwd(4)
    bwd(3)
    give_back(far[2], None)
    act(4)
    bwd(4)
    give_back(far[3], None)
    give_back(near[1], None)
    order = range(len(chunks))
    flat = [k for c in order for k in chunks[c]]
    new_down, new_moment, token = down(
        cap,
        [len(chunks[c]) for c in order],
        ndp,
        dp_idx,
        [p for c in order for p in pieces[c]],
        gotten(flat),
        wd,
        mom,
        mark,
    )
    mark[:] = [token]
    give_back(near[2], None)
    tail = far[1] + near[2] + far[3]
    early = [k for k in flat if k not in tail]
    part, picks = combine(cap, early, tail, me, target, [back[k] for k in early], mark)
    grad_tokens = finish(cap, picks, part, [back[k] for k in tail])
    return (grad_tokens, new_down[None], new_moment[None])


def solution(mesh):
    placed = (
        P("expert", "dp"),
        P("expert", "dp"),
        P("expert", None),
        P("expert", None),
        P("expert", "dp", None),
        P("expert", "dp", None),
        P("expert", None, "dp"),
        P("expert", None, "dp"),
    )
    return jax.shard_map(
        local,
        mesh=mesh,
        in_specs=placed,
        out_specs=(P("expert", "dp"), P("expert", None, "dp"), P("expert", None, "dp")),
        check_vma=False,
    )
```
